256 devices in a mesh: section: 2 (over y_hi), wide: 16 (over y_lo, z), narrow: 8 (over x, core).
Axes of the slice: x: 4, y: 4 (y_hi: 2, y_lo: 2; y = y_hi * 2 + y_lo), z: 8, core: 2. Of those that a mesh axis runs over, the one named last changes fastest.
Arguments:
- saved_inputs: bfloat16 [2, 512, 8192], P('section', None, 'narrow'), may hold values from -6 to 6
- upstream: bfloat16 [512, 8192], P('wide', 'narrow'), may hold values from -6 to 6
- up_weight: bfloat16 [2, 8192, 16384], P('section', 'narrow', 'wide'), may hold values from -0.0625 to 0.0625
- down_weight: bfloat16 [2, 16384, 8192], P('section', 'wide', 'narrow'), may hold values from -0.046875 to 0.046875
Outputs:
- boundary_grads: bfloat16 [2, 512, 8192], P('section', 'wide', 'narrow')
- up_grads: bfloat16 [2, 8192, 16384], P('section', 'narrow', 'wide')
- down_grads: bfloat16 [2, 16384, 8192], P('section', 'wide', 'narrow')
The draws below stay inside these ranges and needn't reach their ends.
All inputs are finite; a program needn't handle non-finite values.
Results may differ from the reference program's by a relative error of at most 0.028.
Values may be sent and summed in bfloat16 or wider, within the bound.
No kernel may reach another device: no remote copies, remote signals or barrier semaphores. Data moves between devices by JAX's collectives and lax.ppermute only.
A program may use at most 64 MiB of HBM per device.

```python
import jax
import jax.numpy as jnp

D = 8192
FF = 16384
TOKENS = 512


def block_scale(own_key, dims, pieces, smallest, largest):
    def one(position, shards_of):
        heights = jax.random.uniform(jax.random.fold_in(jax.random.fold_in(own_key, 6), position), (shards_of,), jnp.float32, smallest / len(pieces), largest / len(pieces))
        return jnp.repeat(jnp.exp(heights), dims[position] // shards_of).reshape((-1,) + (1,) * (len(dims) - position - 1))

    gain = one(*pieces[0])
    for cut in pieces[1:]:
        gain = gain * one(*cut)
    return gain


def gaussian(rng, shape, deviation, limit, split=(), kind=jnp.bfloat16):
    drawn = deviation * jax.random.normal(rng, shape, jnp.float32)
    if split:
        drawn = drawn * block_scale(rng, shape, split, -0.22, 0.18)
    return jnp.clip(drawn, -limit, limit).astype(kind)


def setup_inputs(seed: int = 0) -> dict:
    streams_of = jax.random.split(jax.random.key(seed), 5)
    return {
        "saved_inputs": gaussian(streams_of[0], (2, TOKENS, D), 1.0, 6.0, ((0, 2), (2, 8))),
        "upstream": gaussian(streams_of[1], (TOKENS, D), 1.0, 6.0, ((0, 16), (1, 8))),
        "up_weight": gaussian(streams_of[2], (2, D, FF), D ** -0.5, 0.0625, ((0, 2), (1, 8), (2, 16))),
        "down_weight": gaussian(streams_of[3], (2, FF, D), FF ** -0.5, 0.046875, ((0, 2), (1, 16), (2, 8))),
    }


gelu_scale = 0.7978845608028654
cubic_term = 0.044715


def gelu_parts(pre_act):
    inner = jnp.tanh(gelu_scale * (pre_act + cubic_term * pre_act * pre_act * pre_act))
    act_value = 0.5 * pre_act * (1.0 + inner)
    slopes = 0.5 * (1.0 + inner) + 0.5 * pre_act * (1.0 - inner * inner) * gelu_scale * (1.0 + 3.0 * cubic_term * pre_act * pre_act)
    return act_value, slopes


def layer_back(incoming, saved_rows, w_up, w_down):
    pre_act = jnp.dot(saved_rows, w_up, preferred_element_type=jnp.float32)
    act_value, slopes = gelu_parts(pre_act)
    hidden = act_value.astype(jnp.bfloat16)
    grad_down = jnp.dot(hidden.T, incoming, preferred_element_type=jnp.float32).astype(jnp.bfloat16)
    back_grad = jnp.dot(incoming, w_down.T, preferred_element_type=jnp.float32)
    slope_grad = (back_grad * slopes).astype(jnp.bfloat16)
    grad_up = jnp.dot(saved_rows.T, slope_grad, preferred_element_type=jnp.float32).astype(jnp.bfloat16)
    summed = jnp.dot(slope_grad, w_up.T, preferred_element_type=jnp.float32)
    grad_in = (incoming.astype(jnp.float32) + summed).astype(jnp.bfloat16)
    return grad_in, grad_up, grad_down


def reference(saved_inputs, upstream, up_weight, down_weight):
    upper_in, upper_up, upper_down = layer_back(upstream, saved_inputs[1], up_weight[1], down_weight[1])
    lower_in, lower_up, lower_down = layer_back(upper_in, saved_inputs[0], up_weight[0], down_weight[0])
    return (jnp.stack([lower_in, upper_in]), jnp.stack([lower_up, upper_up]), jnp.stack([lower_down, upper_down]))
```

```python
import jax
import jax.numpy as jnp
from jax import lax
from jax.sharding import Mesh, PartitionSpec as P

gelu_scale = 0.7978845608028654
cubic_term = 0.044715

X, CORES, YLO, Z = 4, 2, 2, 8
WIDE = YLO * Z
CHUNKS = 1
AXES = ("section", "ylo", "z", "x", "core")
WIDE_AXES = ("ylo", "z")


def gelu_parts(pre_act):
    inner = jnp.tanh(gelu_scale * (pre_act + cubic_term * pre_act * pre_act * pre_act))
    act_value = 0.5 * pre_act * (1.0 + inner)
    slopes = 0.5 * (1.0 + inner) + 0.5 * pre_act * (1.0 - inner * inner) * gelu_scale * (
        1.0 + 3.0 * cubic_term * pre_act * pre_act
    )
    return (act_value, slopes)


def contract_rows(first_op, second_op):
    return lax.dot_general(
        first_op, second_op, (((0,), (0,)), ((), ())), preferred_element_type=jnp.float32
    )


def contract_cols(first_op, second_op):
    return lax.dot_general(
        first_op, second_op, (((1,), (1,)), ((), ())), preferred_element_type=jnp.float32
    )


def other_core(block):
    return lax.ppermute(block, "core", [(0, 1), (1, 0)])


def spread_narrow(partial):
    rows, cols = partial.shape
    half = rows // CORES
    core = lax.axis_index("core")
    sent = lax.dynamic_slice_in_dim(partial, (1 - core) * half, half, 0)
    kept = lax.dynamic_slice_in_dim(partial, core * half, half, 0)
    pair = kept.astype(jnp.float32) + other_core(sent).astype(jnp.float32)
    blocks = lax.all_to_all(
        pair.astype(jnp.bfloat16).reshape(X, half // X, cols), "x", 0, 0, tiled=True
    )
    return jnp.sum(blocks.astype(jnp.float32), axis=0)


def gather_narrow(block):
    rows, cols = block.shape
    mine = lax.all_to_all(
        jnp.broadcast_to(block[None], (X, rows, cols)), "x", 0, 0, tiled=True
    ).reshape(X * rows, cols)
    theirs = other_core(mine)
    first = lax.axis_index("core") == 0
    return jnp.concatenate(
        [jnp.where(first, mine, theirs), jnp.where(first, theirs, mine)], axis=0
    )


def spread_wide(partial):
    rows, cols = partial.shape
    blocks = lax.all_to_all(
        partial.reshape(WIDE, rows // WIDE, cols), WIDE_AXES, 0, 0, tiled=True
    )
    return jnp.sum(blocks.astype(jnp.float32), axis=0)


def gather_wide(block):
    rows, cols = block.shape
    return lax.all_to_all(
        jnp.broadcast_to(block[None], (WIDE, rows, cols)), WIDE_AXES, 0, 0, tiled=True
    ).reshape(WIDE * rows, cols)


def chain(own_rows, slope_share, w_up, w_down):
    whole = gather_wide(own_rows)
    back_share = spread_narrow(contract_cols(whole, w_down).astype(jnp.bfloat16))
    slope_part = (back_share * slope_share).astype(jnp.bfloat16)
    slope_grad = gather_narrow(slope_part)
    summed = spread_wide(contract_cols(slope_grad, w_up).astype(jnp.bfloat16))
    grad_in = (own_rows.astype(jnp.float32) + summed).astype(jnp.bfloat16)
    return whole, slope_grad, grad_in


def chunk_rows(block, chunks):
    rows, cols = block.shape
    split = block.reshape(WIDE, chunks, rows // (WIDE * chunks), cols)
    return [split[:, c].reshape(rows // chunks, cols) for c in range(chunks)]


def body(saved_inputs, upstream, up_weight, down_weight):
    saved = chunk_rows(saved_inputs[0], CHUNKS)
    w_up = up_weight[0]
    w_down = down_weight[0]
    step = upstream.shape[0] // CHUNKS
    upper_own = [upstream[c * step : (c + 1) * step] for c in range(CHUNKS)]

    pre = [
        spread_narrow(
            jnp.dot(rows, w_up, preferred_element_type=jnp.float32).astype(jnp.bfloat16)
        )
        for rows in saved
    ]
    parts = [gelu_parts(share) for share in pre]
    hidden = [gather_narrow(act.astype(jnp.bfloat16)) for act, _ in parts]

    upper = [chain(own, part[1], w_up, w_down) for own, part in zip(upper_own, parts)]
    lower_own = [lax.ppermute(out[2], "section", [(1, 0)]) for out in upper]
    lower = [chain(own, part[1], w_up, w_down) for own, part in zip(lower_own, parts)]

    is_upper = lax.axis_index("section") == 1

    def picked(index):
        return jnp.concatenate(
            [jnp.where(is_upper, u[index], l[index]) for u, l in zip(upper, lower)], axis=0
        )

    incoming, slope_grad, grad_in = picked(0), picked(1), picked(2)
    grad_down = contract_rows(jnp.concatenate(hidden, axis=0), incoming).astype(jnp.bfloat16)
    grad_up = contract_rows(jnp.concatenate(saved, axis=0), slope_grad).astype(jnp.bfloat16)
    return grad_in[None], grad_up[None], grad_down[None]


def solution(mesh):
    fine = Mesh(mesh.devices.reshape(2, YLO, Z, X, CORES), AXES)
    wide, narrow = WIDE_AXES, ("x", "core")
    return jax.shard_map(
        body,
        mesh=fine,
        in_specs=(
            P("section", None, narrow),
            P(wide, narrow),
            P("section", narrow, wide),
            P("section", wide, narrow),
        ),
        out_specs=(
            P("section", wide, narrow),
            P("section", narrow, wide),
            P("section", wide, narrow),
        ),
        check_vma=False,
    )
```

```python
import jax
import jax.numpy as jnp
from jax import lax
from jax.sharding import Mesh, PartitionSpec as P

gelu_scale = 0.7978845608028654
cubic_term = 0.044715

X, CORES, YLO, Z = 4, 2, 2, 8
WIDE = YLO * Z
CHUNKS = 2
AXES = ("section", "ylo", "z", "x", "core")
WIDE_AXES = ("ylo", "z")


def gelu_parts(pre_act):
    inner = jnp.tanh(gelu_scale * (pre_act + cubic_term * pre_act * pre_act * pre_act))
    act_value = 0.5 * pre_act * (1.0 + inner)
    slopes = 0.5 * (1.0 + inner) + 0.5 * pre_act * (1.0 - inner * inner) * gelu_scale * (
        1.0 + 3.0 * cubic_term * pre_act * pre_act
    )
    return (act_value, slopes)


def contract(first_op, second_op, first_dim, second_dim):
    return lax.dot_general(
        first_op,
        second_op,
        (((first_dim,), (second_dim,)), ((), ())),
        preferred_element_type=jnp.float32,
    )


def other_core(block):
    return lax.ppermute(block, "core", [(0, 1), (1, 0)])


def halves(weight, dim):
    size = weight.shape[dim] // CORES
    core = lax.axis_index("core")
    return (
        lax.dynamic_slice_in_dim(weight, core * size, size, dim),
        lax.dynamic_slice_in_dim(weight, (1 - core) * size, size, dim),
    )


def in_order(mine, theirs):
    first = lax.axis_index("core") == 0
    return jnp.concatenate(
        [jnp.where(first, mine, theirs), jnp.where(first, theirs, mine)], axis=1
    )


def narrow_total(mine, theirs):
    pair = mine + other_core(theirs.astype(jnp.bfloat16)).astype(jnp.float32)
    sent = pair.astype(jnp.bfloat16)
    total = pair
    for distance in (1, 3, 2):
        route = [(i, (i + distance) % X) for i in range(X)]
        total = total + lax.ppermute(sent, "x", route).astype(jnp.float32)
    return total


def spread_wide(partial):
    rows, cols = partial.shape
    blocks = lax.all_to_all(
        partial.reshape(WIDE, rows // WIDE, cols), WIDE_AXES, 0, 0, tiled=True
    )
    return jnp.sum(blocks.astype(jnp.float32), axis=0)


def gather_wide(block):
    rows, cols = block.shape
    return lax.all_to_all(
        jnp.broadcast_to(block[None], (WIDE, rows, cols)), WIDE_AXES, 0, 0, tiled=True
    ).reshape(WIDE * rows, cols)


def chain(own_rows, slopes, up_halves, down_halves):
    whole = gather_wide(own_rows)
    theirs = contract(whole, down_halves[1], 1, 1)
    mine = contract(whole, down_halves[0], 1, 1)
    slope_mine = (narrow_total(mine, theirs) * slopes).astype(jnp.bfloat16)
    slope_theirs = other_core(slope_mine)
    summed = spread_wide(
        (
            contract(slope_mine, up_halves[0], 1, 1) + contract(slope_theirs, up_halves[1], 1, 1)
        ).astype(jnp.bfloat16)
    )
    grad_in = (own_rows.astype(jnp.float32) + summed).astype(jnp.bfloat16)
    return whole, slope_mine, slope_theirs, grad_in


def chunk_rows(block):
    rows, cols = block.shape
    split = block.reshape(WIDE, CHUNKS, rows // (WIDE * CHUNKS), cols)
    return split.transpose(1, 0, 2, 3).reshape(rows, cols)


def cut(block):
    step = block.shape[0] // CHUNKS
    return [block[c * step : (c + 1) * step] for c in range(CHUNKS)]


def body(saved_inputs, upstream, up_weight, down_weight):
    saved = chunk_rows(saved_inputs[0])
    up_halves = halves(up_weight[0], 1)
    down_halves = halves(down_weight[0], 0)

    theirs = contract(saved, up_halves[1], 1, 0)
    mine = contract(saved, up_halves[0], 1, 0)
    act, slopes = gelu_parts(narrow_total(mine, theirs))
    hidden_mine = act.astype(jnp.bfloat16)
    hidden = in_order(hidden_mine, other_core(hidden_mine))

    upper_own = cut(upstream)
    upper = [chain(own, s, up_halves, down_halves) for own, s in zip(upper_own, cut(slopes))]
    lower_own = [lax.ppermute(out[3], "section", [(1, 0)]) for out in upper]
    lower = [chain(own, s, up_halves, down_halves) for own, s in zip(lower_own, cut(slopes))]

    is_upper = lax.axis_index("section") == 1

    def picked(index):
        return jnp.concatenate(
            [jnp.where(is_upper, u[index], l[index]) for u, l in zip(upper, lower)], axis=0
        )

    grad_down = contract(hidden, picked(0), 0, 0).astype(jnp.bfloat16)
    grad_up = contract(saved, in_order(picked(1), picked(2)), 0, 0).astype(jnp.bfloat16)
    return picked(3)[None], grad_up[None], grad_down[None]


def solution(mesh):
    fine = Mesh(mesh.devices.reshape(2, YLO, Z, X, CORES), AXES)
    wide, narrow = WIDE_AXES, ("x", "core")
    return jax.shard_map(
        body,
        mesh=fine,
        in_specs=(
            P("section", None, narrow),
            P(wide, narrow),
            P("section", narrow, wide),
            P("section", wide, narrow),
        ),
        out_specs=(
            P("section", wide, narrow),
            P("section", narrow, wide),
            P("section", wide, narrow),
        ),
        check_vma=False,
    )
```

```python
import jax
import jax.numpy as jnp
from jax import lax
from jax.sharding import Mesh, PartitionSpec as P

gelu_scale = 0.7978845608028654
cubic_term = 0.044715

X, CORES, YLO, Z = 4, 2, 2, 8
WIDE = YLO * Z
AXES = ("section", "ylo", "z", "x", "core")
WIDE_AXES = ("ylo", "z")
CROSS_AXES = ("section", "ylo")


def gelu_parts(pre_act):
    inner = jnp.tanh(gelu_scale * (pre_act + cubic_term * pre_act * pre_act * pre_act))
    act_value = 0.5 * pre_act * (1.0 + inner)
    slopes = 0.5 * (1.0 + inner) + 0.5 * pre_act * (1.0 - inner * inner) * gelu_scale * (
        1.0 + 3.0 * cubic_term * pre_act * pre_act
    )
    return (act_value, slopes)


def contract(first_op, second_op, first_dim, second_dim):
    return lax.dot_general(
        first_op,
        second_op,
        (((first_dim,), (second_dim,)), ((), ())),
        preferred_element_type=jnp.float32,
    )


def after(value, *others):
    return lax.optimization_barrier((value, others))[0]


def other_core(block):
    return lax.ppermute(block, "core", [(0, 1), (1, 0)])


def to_upper(block):
    return lax.ppermute(block, CROSS_AXES, [(0, 3), (1, 2)])


def to_lower(block):
    return lax.ppermute(block, CROSS_AXES, [(3, 0), (2, 1)])


def halves(weight, dim):
    size = weight.shape[dim] // CORES
    core = lax.axis_index("core")
    return (
        lax.dynamic_slice_in_dim(weight, core * size, size, dim),
        lax.dynamic_slice_in_dim(weight, (1 - core) * size, size, dim),
    )


def in_order(mine, theirs):
    first = lax.axis_index("core") == 0
    return jnp.concatenate(
        [jnp.where(first, mine, theirs), jnp.where(first, theirs, mine)], axis=1
    )


def narrow_total(mine, theirs):
    pair = mine + other_core(theirs.astype(jnp.bfloat16)).astype(jnp.float32)
    sent = pair.astype(jnp.bfloat16)
    total = pair
    for distance in (1, 3, 2):
        route = [(i, (i + distance) % X) for i in range(X)]
        total = total + lax.ppermute(sent, "x", route).astype(jnp.float32)
    return total


def spread_wide(partial):
    rows, cols = partial.shape
    blocks = lax.all_to_all(
        partial.reshape(WIDE, rows // WIDE, cols), WIDE_AXES, 0, 0, tiled=True
    )
    return jnp.sum(blocks.astype(jnp.float32), axis=0)


def gather_wide(block):
    rows, cols = block.shape
    return lax.all_to_all(
        jnp.broadcast_to(block[None], (WIDE, rows, cols)), WIDE_AXES, 0, 0, tiled=True
    ).reshape(WIDE * rows, cols)


def slope_of(whole, down_halves, slopes):
    theirs = contract(whole, down_halves[1], 1, 1)
    mine = contract(whole, down_halves[0], 1, 1)
    slope_mine = (narrow_total(mine, theirs) * slopes).astype(jnp.bfloat16)
    return slope_mine, other_core(slope_mine)


def back_through_up(slope, up_halves):
    return (contract(slope[0], up_halves[0], 1, 1) + contract(slope[1], up_halves[1], 1, 1)).astype(
        jnp.bfloat16
    )


def body(saved_inputs, upstream, up_weight, down_weight):
    is_upper = lax.axis_index("section") == 1

    def pick(upper, lower):
        return jnp.where(is_upper, upper, lower)

    tokens = saved_inputs.shape[1]
    part = upstream.shape[0] // 2
    by_part = saved_inputs[0].reshape(WIDE, 2, part, -1)
    saved = [by_part[:, c].reshape(tokens // 2, -1) for c in range(2)]
    w_up, w_down = up_weight[0], down_weight[0]
    up_halves, down_halves = halves(w_up, 1), halves(w_down, 0)

    early, late = upstream[:part], upstream[part:]
    gathered = gather_wide(pick(early, late))
    sent_down = to_upper(w_down)
    top = [gathered, to_upper(gathered)]

    hidden, slopes = [], []
    for rows in saved:
        theirs = contract(rows, up_halves[1], 1, 0)
        mine = contract(rows, up_halves[0], 1, 0)
        act, slope = gelu_parts(narrow_total(mine, theirs))
        act = act.astype(jnp.bfloat16)
        hidden.append((act, other_core(act)))
        slopes.append(slope)
    lower_slopes = pick(to_upper(slopes[1].astype(jnp.bfloat16)).astype(jnp.float32), slopes[0])

    top_slopes = [slope_of(top[0], down_halves, slopes[0])]
    moved = to_lower(back_through_up(top_slopes[0], up_halves))
    sent_up = to_upper(after(w_up, sent_down))
    top_slopes.append(slope_of(top[1], down_halves, slopes[1]))
    summed = spread_wide(pick(back_through_up(top_slopes[1], up_halves), moved))
    middle = (pick(late, early).astype(jnp.float32) + summed).astype(jnp.bfloat16)

    low = gather_wide(middle)
    low_down = halves(pick(sent_down, w_down), 0)
    low_up = halves(pick(sent_up, w_up), 1)
    low_slope = slope_of(low, low_down, lower_slopes)
    low_summed = spread_wide(back_through_up(low_slope, low_up))
    bottom = (middle.astype(jnp.float32) + low_summed).astype(jnp.bfloat16)

    swap = [(0, 1), (1, 0)]
    upper_first = lax.ppermute(middle, "section", swap)
    lower_last = lax.ppermute(bottom, "section", swap)
    low_rest = to_lower(low)
    low_slope_rest = [to_lower(block) for block in low_slope]

    grad_in = jnp.concatenate([pick(upper_first, bottom), pick(middle, lower_last)], axis=0)
    incoming = jnp.concatenate([pick(top[0], low), pick(top[1], low_rest)], axis=0)
    slope_grad = jnp.concatenate(
        [
            in_order(*[pick(u, l) for u, l in zip(top_slopes[0], low_slope)]),
            in_order(*[pick(u, l) for u, l in zip(top_slopes[1], low_slope_rest)]),
        ],
        axis=0,
    )
    hidden = jnp.concatenate([in_order(*block) for block in hidden], axis=0)
    grad_down = contract(hidden, incoming, 0, 0).astype(jnp.bfloat16)
    grad_up = contract(jnp.concatenate(saved, axis=0), slope_grad, 0, 0).astype(jnp.bfloat16)
    return grad_in[None], grad_up[None], grad_down[None]


def solution(mesh):
    fine = Mesh(mesh.devices.reshape(2, YLO, Z, X, CORES), AXES)
    wide, narrow = WIDE_AXES, ("x", "core")
    return jax.shard_map(
        body,
        mesh=fine,
        in_specs=(
            P("section", None, narrow),
            P(wide, narrow),
            P("section", narrow, wide),
            P("section", wide, narrow),
        ),
        out_specs=(
            P("section", wide, narrow),
            P("section", narrow, wide),
            P("section", wide, narrow),
        ),
        check_vma=False,
    )
```

```python
import jax
import jax.numpy as jnp
from jax import lax
from jax.sharding import Mesh, PartitionSpec as P

gelu_scale = 0.7978845608028654
cubic_term = 0.044715

X, CORES, YLO, Z = 4, 2, 2, 8
WIDE = YLO * Z
AXES = ("section", "ylo", "z", "x", "core")
WIDE_AXES = ("ylo", "z")
CROSS_AXES = ("section", "ylo")


def gelu_parts(pre_act):
    inner = jnp.tanh(gelu_scale * (pre_act + cubic_term * pre_act * pre_act * pre_act))
    act_value = 0.5 * pre_act * (1.0 + inner)
    slopes = 0.5 * (1.0 + inner) + 0.5 * pre_act * (1.0 - inner * inner) * gelu_scale * (
        1.0 + 3.0 * cubic_term * pre_act * pre_act
    )
    return (act_value, slopes)


def contract(first_op, second_op, first_dim, second_dim):
    return lax.dot_general(
        first_op,
        second_op,
        (((first_dim,), (second_dim,)), ((), ())),
        preferred_element_type=jnp.float32,
    )


def together(*values):
    return lax.optimization_barrier(values)


def after(value, *others):
    return together(value, *others)[0]


def other_core(block):
    return lax.ppermute(block, "core", [(0, 1), (1, 0)])


def to_upper(block):
    return lax.ppermute(block, CROSS_AXES, [(0, 3), (1, 2)])


def to_lower(block):
    return lax.ppermute(block, CROSS_AXES, [(3, 0), (2, 1)])


def halves(weight, dim):
    size = weight.shape[dim] // CORES
    core = lax.axis_index("core")
    return (
        lax.dynamic_slice_in_dim(weight, core * size, size, dim),
        lax.dynamic_slice_in_dim(weight, (1 - core) * size, size, dim),
    )


def in_order(mine, theirs):
    first = lax.axis_index("core") == 0
    return jnp.concatenate(
        [jnp.where(first, mine, theirs), jnp.where(first, theirs, mine)], axis=1
    )


def narrow_total(mine, theirs):
    pair = mine + other_core(theirs.astype(jnp.bfloat16)).astype(jnp.float32)
    sent = pair.astype(jnp.bfloat16)
    total = pair
    for distance in (1, 3, 2):
        route = [(i, (i + distance) % X) for i in range(X)]
        total = total + lax.ppermute(sent, "x", route).astype(jnp.float32)
    return total


def spread_wide(partial):
    rows, cols = partial.shape
    return lax.all_to_all(
        partial.reshape(WIDE, rows // WIDE, cols), WIDE_AXES, 0, 0, tiled=True
    )


def add_blocks(blocks):
    return jnp.sum(blocks.astype(jnp.float32), axis=0)


def gather_wide(block):
    rows, cols = block.shape
    return lax.all_to_all(
        jnp.broadcast_to(block[None], (WIDE, rows, cols)), WIDE_AXES, 0, 0, tiled=True
    ).reshape(WIDE * rows, cols)


def back_total(whole, down_halves):
    theirs = contract(whole, down_halves[1], 1, 1)
    mine = contract(whole, down_halves[0], 1, 1)
    return narrow_total(mine, theirs)


def slope_of(total, slopes):
    mine = (total * slopes).astype(jnp.bfloat16)
    return mine, other_core(mine)


def back_through_up(slope, up_halves):
    return (contract(slope[0], up_halves[0], 1, 1) + contract(slope[1], up_halves[1], 1, 1)).astype(
        jnp.bfloat16
    )


def body(saved_inputs, upstream, up_weight, down_weight):
    is_upper = lax.axis_index("section") == 1

    def pick(upper, lower):
        return jnp.where(is_upper, upper, lower)

    tokens = saved_inputs.shape[1]
    part = upstream.shape[0] // 2
    by_part = saved_inputs[0].reshape(WIDE, 2, part, -1)
    saved = [by_part[:, c].reshape(tokens // 2, -1) for c in range(2)]
    w_up, w_down = up_weight[0], down_weight[0]
    up_halves, down_halves = halves(w_up, 1), halves(w_down, 0)

    half = w_down.shape[0] // 2
    down_pieces = [to_upper(w_down[:half])]

    early, late = upstream[:part], upstream[part:]
    gathered = gather_wide(pick(early, late))

    def pre_total(rows):
        theirs = contract(rows, up_halves[1], 1, 0)
        mine = contract(rows, up_halves[0], 1, 0)
        return narrow_total(mine, theirs)

    hidden, slopes = [], []

    def keep(total):
        act, slope = gelu_parts(total)
        act = act.astype(jnp.bfloat16)
        hidden.append((act, other_core(act)))
        slopes.append(slope)

    keep(pre_total(saved[0]))
    gathered, *down_pieces = together(gathered, *down_pieces)
    top_total = back_total(gathered, down_halves)
    top_total, top_rest = together(top_total, to_upper(gathered))
    top_slope = slope_of(top_total, slopes[0])
    top_slope, late_total = together(top_slope, pre_total(after(saved[1], gathered)))
    keep(late_total)
    moved = to_lower(back_through_up(top_slope, up_halves))
    rest_total = back_total(top_rest, down_halves)
    rest_total, piece = together(rest_total, to_upper(after(w_down[half:], top_rest)))
    down_pieces.append(piece)
    top_slope_rest = slope_of(rest_total, slopes[1])
    partial = pick(back_through_up(top_slope_rest, up_halves), moved)
    blocks, lower_slopes, *up_pieces = together(
        spread_wide(partial),
        to_upper(after(slopes[1].astype(jnp.bfloat16), rest_total)),
        to_upper(after(w_up[:half], rest_total)),
    )
    lower_slopes = pick(lower_slopes.astype(jnp.float32), slopes[0])
    middle = (pick(late, early).astype(jnp.float32) + add_blocks(blocks)).astype(jnp.bfloat16)
    up_pieces.append(to_upper(after(w_up[half:], blocks)))

    hidden = jnp.concatenate([in_order(*block) for block in hidden], axis=0)
    low_down = pick(jnp.concatenate(down_pieces, axis=0), w_down)
    low, hidden, low_down = together(gather_wide(middle), hidden, low_down)
    low_rest = to_lower(low)
    low_total = back_total(low, halves(low_down, 0))
    incoming = jnp.concatenate([pick(gathered, low), pick(top_rest, low_rest)], axis=0)
    grad_down = contract(hidden, incoming, 0, 0).astype(jnp.bfloat16)
    low_up = pick(jnp.concatenate(up_pieces, axis=0), w_up)
    low_total, grad_down, low_up = together(low_total, grad_down, low_up)
    low_slope = slope_of(low_total, lower_slopes)
    low_slope_rest = to_lower(low_slope[0])
    low_blocks = spread_wide(back_through_up(low_slope, halves(low_up, 1)))
    slope_grad = jnp.concatenate(
        [
            in_order(*[pick(u, l) for u, l in zip(top_slope, low_slope)]),
            in_order(
                pick(top_slope_rest[0], low_slope_rest),
                pick(top_slope_rest[1], other_core(low_slope_rest)),
            ),
        ],
        axis=0,
    )
    grad_up = contract(jnp.concatenate(saved, axis=0), slope_grad, 0, 0).astype(jnp.bfloat16)
    low_blocks, grad_up = together(low_blocks, grad_up)
    bottom = (middle.astype(jnp.float32) + add_blocks(low_blocks)).astype(jnp.bfloat16)

    swap = [(0, 1), (1, 0)]
    upper_first = lax.ppermute(middle, "section", swap)
    lower_last = lax.ppermute(bottom, "section", swap)
    grad_in = jnp.concatenate([pick(upper_first, bottom), pick(middle, lower_last)], axis=0)
    return grad_in[None], grad_up[None], grad_down[None]


def solution(mesh):
    fine = Mesh(mesh.devices.reshape(2, YLO, Z, X, CORES), AXES)
    wide, narrow = WIDE_AXES, ("x", "core")
    return jax.shard_map(
        body,
        mesh=fine,
        in_specs=(
            P("section", None, narrow),
            P(wide, narrow),
            P("section", narrow, wide),
            P("section", wide, narrow),
        ),
        out_specs=(
            P("section", wide, narrow),
            P("section", narrow, wide),
            P("section", wide, narrow),
        ),
        check_vma=False,
    )
```

```python
import jax
import jax.numpy as jnp
from jax import lax
from jax.sharding import Mesh, PartitionSpec as P

gelu_scale = 0.7978845608028654
cubic_term = 0.044715

X, CORES, YLO, Z = 4, 2, 2, 8
WIDE = YLO * Z
AXES = ("section", "ylo", "z", "x", "core")
WIDE_AXES = ("ylo", "z")
CROSS_AXES = ("section", "ylo")


def gelu_parts(pre_act):
    inner = jnp.tanh(gelu_scale * (pre_act + cubic_term * pre_act * pre_act * pre_act))
    act_value = 0.5 * pre_act * (1.0 + inner)
    slopes = 0.5 * (1.0 + inner) + 0.5 * pre_act * (1.0 - inner * inner) * gelu_scale * (
        1.0 + 3.0 * cubic_term * pre_act * pre_act
    )
    return (act_value, slopes)


def contract(first_op, second_op, first_dim, second_dim):
    return lax.dot_general(
        first_op,
        second_op,
        (((first_dim,), (second_dim,)), ((), ())),
        preferred_element_type=jnp.float32,
    )


def together(*values):
    return lax.optimization_barrier(values)


def other_core(block):
    return lax.ppermute(block, "core", [(0, 1), (1, 0)])


def to_upper(block):
    return lax.ppermute(block, CROSS_AXES, [(0, 3), (1, 2)])


def to_lower(block):
    return lax.ppermute(block, CROSS_AXES, [(3, 0), (2, 1)])


def halves(weight, dim):
    size = weight.shape[dim] // CORES
    core = lax.axis_index("core")
    return (
        lax.dynamic_slice_in_dim(weight, core * size, size, dim),
        lax.dynamic_slice_in_dim(weight, (1 - core) * size, size, dim),
    )


def in_order(mine, theirs):
    first = lax.axis_index("core") == 0
    return jnp.concatenate(
        [jnp.where(first, mine, theirs), jnp.where(first, theirs, mine)], axis=1
    )


def narrow_terms(mine, theirs):
    pair = mine + other_core(theirs.astype(jnp.bfloat16)).astype(jnp.float32)
    sent = pair.astype(jnp.bfloat16)
    routes = [[(i, (i + distance) % X) for i in range(X)] for distance in (1, 3, 2)]
    return [pair] + [lax.ppermute(sent, "x", route) for route in routes]


def add_terms(terms):
    return sum(term.astype(jnp.float32) for term in terms)


def spread_wide(partial):
    rows, cols = partial.shape
    return lax.all_to_all(
        partial.reshape(WIDE, rows // WIDE, cols), WIDE_AXES, 0, 0, tiled=True
    )


def add_blocks(blocks):
    return jnp.sum(blocks.astype(jnp.float32), axis=0)


def gather_wide(block):
    rows, cols = block.shape
    return lax.all_to_all(
        jnp.broadcast_to(block[None], (WIDE, rows, cols)), WIDE_AXES, 0, 0, tiled=True
    ).reshape(WIDE * rows, cols)


def back_total(whole, down_halves):
    theirs = contract(whole, down_halves[1], 1, 1)
    mine = contract(whole, down_halves[0], 1, 1)
    return add_terms(narrow_terms(mine, theirs))


def slope_of(total, slopes):
    mine = (total * slopes).astype(jnp.bfloat16)
    return mine, other_core(mine)


def back_through_up(slope, up_halves):
    return (contract(slope[0], up_halves[0], 1, 1) + contract(slope[1], up_halves[1], 1, 1)).astype(
        jnp.bfloat16
    )


def body(saved_inputs, upstream, up_weight, down_weight):
    is_upper = lax.axis_index("section") == 1

    def pick(upper, lower):
        return jnp.where(is_upper, upper, lower)

    def by_part(block):
        rows, cols = block.shape
        split = block.reshape(WIDE, 2, rows // (2 * WIDE), cols)
        return [split[:, c].reshape(rows // 2, cols) for c in range(2)]

    w_up, w_down = up_weight[0], down_weight[0]
    up_halves, down_halves = halves(w_up, 1), halves(w_down, 0)
    saved = by_part(saved_inputs[0])
    first, last = slice(0, saved[0].shape[0]), slice(saved[0].shape[0], None)

    sent_down = to_upper(w_down)

    theirs = jnp.concatenate([contract(rows, up_halves[1], 1, 0) for rows in saved], axis=0)
    mine = jnp.concatenate([contract(rows, up_halves[0], 1, 0) for rows in saved], axis=0)
    pre = narrow_terms(mine, theirs)
    gathered, pre[1], pre[2] = together(gather_wide(upstream), pre[1], pre[2])
    act, slopes = gelu_parts(add_terms(pre))
    act = act.astype(jnp.bfloat16)
    hidden = in_order(act, other_core(act))

    top = by_part(gathered)
    top_slope = slope_of(back_total(top[0], down_halves), slopes[first])
    moved = to_lower(back_through_up(top_slope, up_halves))
    late_slopes, _ = together(slopes[last], top_slope[0])
    top_slope_rest = slope_of(back_total(top[1], down_halves), late_slopes)
    blocks = spread_wide(pick(back_through_up(top_slope_rest, up_halves), moved))
    sent_up = to_upper(together(w_up, sent_down)[0])
    part = upstream.shape[0] // 2
    middle = (
        pick(upstream[part:], upstream[:part]).astype(jnp.float32) + add_blocks(blocks)
    ).astype(jnp.bfloat16)

    low_down = pick(sent_down, w_down)
    low_up = pick(sent_up, w_up)
    lower_slopes = to_upper(slopes[last].astype(jnp.bfloat16))
    low, hidden, low_down, lower_slopes = together(
        gather_wide(middle), hidden, low_down, lower_slopes
    )
    lower_slopes = pick(lower_slopes.astype(jnp.float32), slopes[first])
    low_rest = to_lower(low)
    low_total = back_total(low, halves(low_down, 0))
    incoming = jnp.concatenate([pick(top[0], low), pick(top[1], low_rest)], axis=0)
    grad_down = contract(hidden, incoming, 0, 0).astype(jnp.bfloat16)
    low_total, grad_down, low_up = together(low_total, grad_down, low_up)
    low_slope = slope_of(low_total, lower_slopes)
    low_slope_rest = to_lower(low_slope[0])
    low_blocks = spread_wide(back_through_up(low_slope, halves(low_up, 1)))
    slope_grad = jnp.concatenate(
        [
            in_order(*[pick(u, l) for u, l in zip(top_slope, low_slope)]),
            in_order(
                pick(top_slope_rest[0], low_slope_rest),
                pick(top_slope_rest[1], other_core(low_slope_rest)),
            ),
        ],
        axis=0,
    )
    grad_up = contract(jnp.concatenate(saved, axis=0), slope_grad, 0, 0).astype(jnp.bfloat16)
    low_blocks, grad_up = together(low_blocks, grad_up)
    bottom = (middle.astype(jnp.float32) + add_blocks(low_blocks)).astype(jnp.bfloat16)

    swap = [(0, 1), (1, 0)]
    upper_first = lax.ppermute(middle, "section", swap)
    lower_last = lax.ppermute(bottom, "section", swap)
    grad_in = jnp.concatenate([pick(upper_first, bottom), pick(middle, lower_last)], axis=0)
    return grad_in[None], grad_up[None], grad_down[None]


def solution(mesh):
    fine = Mesh(mesh.devices.reshape(2, YLO, Z, X, CORES), AXES)
    wide, narrow = WIDE_AXES, ("x", "core")
    return jax.shard_map(
        body,
        mesh=fine,
        in_specs=(
            P("section", None, narrow),
            P(wide, narrow),
            P("section", narrow, wide),
            P("section", wide, narrow),
        ),
        out_specs=(
            P("section", wide, narrow),
            P("section", narrow, wide),
            P("section", wide, narrow),
        ),
        check_vma=False,
    )
```

```python
import jax
import jax.numpy as jnp
from jax import lax
from jax.sharding import Mesh, PartitionSpec as P

gelu_scale = 0.7978845608028654
cubic_term = 0.044715

X, CORES, YLO, Z = 4, 2, 2, 8
WIDE = YLO * Z
AXES = ("section", "ylo", "z", "x", "core")
WIDE_AXES = ("ylo", "z")
CROSS_AXES = ("section", "ylo")


def gelu_parts(pre_act):
    inner = jnp.tanh(gelu_scale * (pre_act + cubic_term * pre_act * pre_act * pre_act))
    act_value = 0.5 * pre_act * (1.0 + inner)
    slopes = 0.5 * (1.0 + inner) + 0.5 * pre_act * (1.0 - inner * inner) * gelu_scale * (
        1.0 + 3.0 * cubic_term * pre_act * pre_act
    )
    return (act_value, slopes)


def contract(first_op, second_op, first_dim, second_dim):
    return lax.dot_general(
        first_op,
        second_op,
        (((first_dim,), (second_dim,)), ((), ())),
        preferred_element_type=jnp.float32,
    )


def together(*values):
    return lax.optimization_barrier(values)


def other_core(block):
    return lax.ppermute(block, "core", [(0, 1), (1, 0)])


def to_upper(block):
    return lax.ppermute(block, CROSS_AXES, [(0, 3), (1, 2)])


def to_lower(block):
    return lax.ppermute(block, CROSS_AXES, [(3, 0), (2, 1)])


def halves(weight, dim):
    size = weight.shape[dim] // CORES
    core = lax.axis_index("core")
    return (
        lax.dynamic_slice_in_dim(weight, core * size, size, dim),
        lax.dynamic_slice_in_dim(weight, (1 - core) * size, size, dim),
    )


def in_order(mine, theirs):
    first = lax.axis_index("core") == 0
    return jnp.concatenate(
        [jnp.where(first, mine, theirs), jnp.where(first, theirs, mine)], axis=1
    )


def pair_sum(mine, theirs):
    return mine + other_core(theirs.astype(jnp.bfloat16)).astype(jnp.float32)


def spread_x(partial):
    rows, cols = partial.shape
    blocks = lax.all_to_all(
        partial.astype(jnp.bfloat16).reshape(X, rows // X, cols), "x", 0, 0, tiled=True
    )
    return jnp.sum(blocks.astype(jnp.float32), axis=0)


def gather_x(block):
    rows, cols = block.shape
    return lax.all_to_all(
        jnp.broadcast_to(block[None], (X, rows, cols)), "x", 0, 0, tiled=True
    ).reshape(X * rows, cols)


def step_x(block, distance):
    return lax.ppermute(block, "x", [(i, (i + distance) % X) for i in range(X)])


def spread_x_beside(partial):
    rows, cols = partial.shape
    x = lax.axis_index("x")
    blocks = partial.reshape(X, rows // X, cols)
    total = lax.dynamic_index_in_dim(blocks, x, 0, keepdims=False)
    sent = blocks.astype(jnp.bfloat16)
    for distance in (1, 3, 2):
        target = lax.rem(x + distance, X)
        block = lax.dynamic_index_in_dim(sent, target, 0, keepdims=False)
        total = total + step_x(block, distance).astype(jnp.float32)
    return total


def gather_x_beside(block):
    rows, cols = block.shape
    found = [block] + [step_x(block, X - distance) for distance in (1, 2, 3)]
    twice = jnp.stack(found + found[:-1])
    start = lax.rem(X - lax.axis_index("x"), X)
    return lax.dynamic_slice_in_dim(twice, start, X, 0).reshape(X * rows, cols)


def spread_wide(partial):
    rows, cols = partial.shape
    return lax.all_to_all(
        partial.reshape(WIDE, rows // WIDE, cols), WIDE_AXES, 0, 0, tiled=True
    )


def add_blocks(blocks):
    return jnp.sum(blocks.astype(jnp.float32), axis=0)


def gather_wide(block):
    rows, cols = block.shape
    return lax.all_to_all(
        jnp.broadcast_to(block[None], (WIDE, rows, cols)), WIDE_AXES, 0, 0, tiled=True
    ).reshape(WIDE * rows, cols)


def back_share(whole, down_halves):
    theirs = contract(whole, down_halves[1], 1, 1)
    mine = contract(whole, down_halves[0], 1, 1)
    return spread_x(pair_sum(mine, theirs))


def back_through_up(slope, up_halves):
    return (contract(slope[0], up_halves[0], 1, 1) + contract(slope[1], up_halves[1], 1, 1)).astype(
        jnp.bfloat16
    )


def body(saved_inputs, upstream, up_weight, down_weight):
    is_upper = lax.axis_index("section") == 1

    def pick(upper, lower):
        return jnp.where(is_upper, upper, lower)

    part = upstream.shape[0] // 2

    def part_of(block, index):
        rows, cols = block.shape
        split = block.reshape(rows // (2 * part), 2, part, cols)
        return split[:, index].reshape(rows // 2, cols)

    def both_parts(early, late):
        rows, cols = early.shape
        pair = [block.reshape(rows // part, part, cols) for block in (early, late)]
        return jnp.stack(pair, axis=1).reshape(2 * rows, cols)

    saved = saved_inputs[0]
    w_up, w_down = up_weight[0], down_weight[0]
    up_halves, down_halves = halves(w_up, 1), halves(w_down, 0)

    depth = w_down.shape[0]
    some = w_up.shape[0] // 2
    most = to_upper(jnp.concatenate([w_down, w_up[:some]], axis=0))

    theirs = contract(saved, up_halves[1], 1, 0)
    mine = contract(saved, up_halves[0], 1, 0)
    pre = spread_x_beside(pair_sum(mine, theirs))
    gathered, pre = together(gather_wide(upstream), pre)
    act, slopes = gelu_parts(pre)

    top_mine = gather_x((back_share(gathered, down_halves) * slopes).astype(jnp.bfloat16))
    top_slope = [part_of(top_mine, c) for c in range(2)]
    top_slope = [(block, other_core(block)) for block in top_slope]
    moved = to_lower(back_through_up(top_slope[0], up_halves))
    partial = pick(back_through_up(top_slope[1], up_halves), moved)
    partial, act = together(partial, act.astype(jnp.bfloat16))
    blocks = spread_wide(partial)
    middle = (
        pick(upstream[part:], upstream[:part]).astype(jnp.float32) + add_blocks(blocks)
    ).astype(jnp.bfloat16)

    rest = to_upper(together(w_up[some:], most, blocks)[0])
    low_down = pick(most[:depth], w_down)
    lower_slopes = to_upper(part_of(slopes, 1).astype(jnp.bfloat16))
    hidden = gather_x_beside(act)
    low, hidden, low_down, lower_slopes = together(
        gather_wide(middle), hidden, low_down, lower_slopes
    )
    hidden = in_order(hidden, other_core(hidden))
    lower_slopes = pick(lower_slopes.astype(jnp.float32), part_of(slopes, 0))
    low_rest = to_lower(low)
    low_share = back_share(low, halves(low_down, 0))
    incoming = pick(gathered, both_parts(low, low_rest))
    grad_down = contract(hidden, incoming, 0, 0).astype(jnp.bfloat16)
    low_share, rest = together(low_share, rest)
    low_mine = gather_x((low_share * lower_slopes).astype(jnp.bfloat16))
    low_up = [pick(most[depth:], w_up[:some]), pick(rest, w_up[some:])]
    low_mine, grad_down, *low_up = together(low_mine, grad_down, *low_up)
    low_slope = (low_mine, other_core(low_mine))
    low_slope_rest = to_lower(low_mine)
    low_blocks = spread_wide(
        jnp.concatenate([back_through_up(low_slope, halves(piece, 1)) for piece in low_up], axis=1)
    )
    slope_grad = both_parts(
        in_order(*[pick(u, l) for u, l in zip(top_slope[0], low_slope)]),
        in_order(
            pick(top_slope[1][0], low_slope_rest),
            pick(top_slope[1][1], other_core(low_slope_rest)),
        ),
    )
    grad_up = contract(saved, slope_grad, 0, 0).astype(jnp.bfloat16)
    low_blocks, grad_up = together(low_blocks, grad_up)
    bottom = (middle.astype(jnp.float32) + add_blocks(low_blocks)).astype(jnp.bfloat16)

    swap = [(0, 1), (1, 0)]
    upper_first = lax.ppermute(middle, "section", swap)
    lower_last = lax.ppermute(bottom, "section", swap)
    grad_in = jnp.concatenate([pick(upper_first, bottom), pick(middle, lower_last)], axis=0)
    return grad_in[None], grad_up[None], grad_down[None]


def solution(mesh):
    fine = Mesh(mesh.devices.reshape(2, YLO, Z, X, CORES), AXES)
    wide, narrow = WIDE_AXES, ("x", "core")
    return jax.shard_map(
        body,
        mesh=fine,
        in_specs=(
            P("section", None, narrow),
            P(wide, narrow),
            P("section", narrow, wide),
            P("section", wide, narrow),
        ),
        out_specs=(
            P("section", wide, narrow),
            P("section", narrow, wide),
            P("section", wide, narrow),
        ),
        check_vma=False,
    )
```

```python
import jax
import jax.numpy as jnp
from jax import lax
from jax.sharding import Mesh, PartitionSpec as P

gelu_scale = 0.7978845608028654
cubic_term = 0.044715

X, CORES, YLO, Z = 4, 2, 2, 8
WIDE = YLO * Z
AXES = ("section", "ylo", "z", "x", "core")
WIDE_AXES = ("ylo", "z")
CROSS_AXES = ("section", "ylo")


def gelu_parts(pre_act):
    inner = jnp.tanh(gelu_scale * (pre_act + cubic_term * pre_act * pre_act * pre_act))
    act_value = 0.5 * pre_act * (1.0 + inner)
    slopes = 0.5 * (1.0 + inner) + 0.5 * pre_act * (1.0 - inner * inner) * gelu_scale * (
        1.0 + 3.0 * cubic_term * pre_act * pre_act
    )
    return (act_value, slopes)


def contract(first_op, second_op, first_dim, second_dim):
    return lax.dot_general(
        first_op,
        second_op,
        (((first_dim,), (second_dim,)), ((), ())),
        preferred_element_type=jnp.float32,
    )


def together(*values):
    return lax.optimization_barrier(values)


def other_core(block):
    return lax.ppermute(block, "core", [(0, 1), (1, 0)])


def to_upper(block):
    return lax.ppermute(block, CROSS_AXES, [(0, 3), (1, 2)])


def pair_weights(block):
    pairs = [[0, 3], [1, 2]]
    return lax.all_gather(block, CROSS_AXES, axis=0, tiled=True, axis_index_groups=pairs)


def to_lower(block):
    return lax.ppermute(block, CROSS_AXES, [(3, 0), (2, 1)])


def halves(weight, dim, depth=None):
    rows, cols = depth or weight.shape[0], weight.shape[1]
    core = lax.axis_index("core")

    def half(index):
        if dim == 0:
            return lax.dynamic_slice(weight, (index * (rows // CORES), 0), (rows // CORES, cols))
        return lax.dynamic_slice(weight, (0, index * (cols // CORES)), (rows, cols // CORES))

    return half(core), half(1 - core)


def in_order(mine, theirs):
    first = lax.axis_index("core") == 0
    return jnp.concatenate(
        [jnp.where(first, mine, theirs), jnp.where(first, theirs, mine)], axis=1
    )


def pair_sum(mine, theirs):
    return mine + other_core(theirs.astype(jnp.bfloat16)).astype(jnp.float32)


def spread_x(partial):
    rows, cols = partial.shape
    blocks = lax.all_to_all(
        partial.astype(jnp.bfloat16).reshape(X, rows // X, cols), "x", 0, 0, tiled=True
    )
    return jnp.sum(blocks.astype(jnp.float32), axis=0)


def gather_x(block):
    rows, cols = block.shape
    return lax.all_to_all(
        jnp.broadcast_to(block[None], (X, rows, cols)), "x", 0, 0, tiled=True
    ).reshape(X * rows, cols)


def step_x(block, distance):
    return lax.ppermute(block, "x", [(i, (i + distance) % X) for i in range(X)])


def spread_x_beside(partial):
    rows, cols = partial.shape
    x = lax.axis_index("x")
    blocks = partial.reshape(X, rows // X, cols)
    total = lax.dynamic_index_in_dim(blocks, x, 0, keepdims=False)
    sent = blocks.astype(jnp.bfloat16)
    for distance in (1, 3, 2):
        target = lax.rem(x + distance, X)
        block = lax.dynamic_index_in_dim(sent, target, 0, keepdims=False)
        total = total + step_x(block, distance).astype(jnp.float32)
    return total


def gather_x_beside(block):
    rows, cols = block.shape
    found = [block] + [step_x(block, X - distance) for distance in (1, 2, 3)]
    twice = jnp.stack(found + found[:-1])
    start = lax.rem(X - lax.axis_index("x"), X)
    return lax.dynamic_slice_in_dim(twice, start, X, 0).reshape(X * rows, cols)


def spread_wide(partial):
    rows, cols = partial.shape
    return lax.all_to_all(
        partial.reshape(WIDE, rows // WIDE, cols), WIDE_AXES, 0, 0, tiled=True
    )


def add_blocks(blocks):
    return jnp.sum(blocks.astype(jnp.float32), axis=0)


def gather_wide(block):
    rows, cols = block.shape
    return lax.all_to_all(
        jnp.broadcast_to(block[None], (WIDE, rows, cols)), WIDE_AXES, 0, 0, tiled=True
    ).reshape(WIDE * rows, cols)


def back_share(whole, down_halves):
    theirs = contract(whole, down_halves[1], 1, 1)
    mine = contract(whole, down_halves[0], 1, 1)
    return spread_x(pair_sum(mine, theirs))


def back_through_up(slope, up_halves):
    return (contract(slope[0], up_halves[0], 1, 1) + contract(slope[1], up_halves[1], 1, 1)).astype(
        jnp.bfloat16
    )


def body(saved_inputs, upstream, up_weight, down_weight):
    is_upper = lax.axis_index("section") == 1

    def pick(upper, lower):
        return jnp.where(is_upper, upper, lower)

    part = upstream.shape[0] // 2

    def part_of(block, index):
        rows, cols = block.shape
        split = block.reshape(rows // (2 * part), 2, part, cols)
        return split[:, index].reshape(rows // 2, cols)

    def both_parts(early, late):
        rows, cols = early.shape
        pair = [block.reshape(rows // part, part, cols) for block in (early, late)]
        return jnp.stack(pair, axis=1).reshape(2 * rows, cols)

    saved = saved_inputs[0]
    w_up, w_down = up_weight[0], down_weight[0]
    up_halves, down_halves = halves(w_up, 1), halves(w_down, 0)

    low_down = pair_weights(w_down)

    theirs = contract(saved, up_halves[1], 1, 0)
    mine = contract(saved, up_halves[0], 1, 0)
    pre = spread_x_beside(pair_sum(mine, theirs))
    act, slopes = gelu_parts(pre)
    act = act.astype(jnp.bfloat16)
    slopes = [part_of(slopes, c) for c in range(2)]
    gathered, act, *slopes = together(gather_wide(upstream), act, *slopes)
    low_up = pair_weights(together(w_up, act)[0])

    share = back_share(gathered, down_halves)
    top_mine = [
        gather_x((part_of(share, c) * slopes[c]).astype(jnp.bfloat16)) for c in range(2)
    ]
    top_slope = [(block, other_core(block)) for block in top_mine]
    moved = to_lower(back_through_up(top_slope[0], up_halves))
    partial = pick(back_through_up(top_slope[1], up_halves), moved)
    partial, act, sent = together(partial, act, slopes[1].astype(jnp.bfloat16))
    blocks = spread_wide(partial)
    middle = (
        pick(upstream[part:], upstream[:part]).astype(jnp.float32) + add_blocks(blocks)
    ).astype(jnp.bfloat16)

    hidden = gather_x_beside(act)
    low, hidden, sent = together(gather_wide(middle), hidden, to_upper(sent))
    hidden = in_order(hidden, other_core(hidden))
    low_rest = to_lower(low)
    low_share = back_share(low, halves(low_down, 0, w_down.shape[0]))
    incoming = pick(gathered, both_parts(low, low_rest))
    grad_down = contract(hidden, incoming, 0, 0).astype(jnp.bfloat16)
    low_mine = gather_x(
        (low_share * pick(sent.astype(jnp.float32), slopes[0])).astype(jnp.bfloat16)
    )
    low_mine, grad_down = together(low_mine, grad_down)
    low_slope = (low_mine, other_core(low_mine))
    low_slope_rest = to_lower(low_mine)
    low_blocks = spread_wide(back_through_up(low_slope, halves(low_up, 1, w_up.shape[0])))
    slope_grad = both_parts(
        in_order(*[pick(u, l) for u, l in zip(top_slope[0], low_slope)]),
        in_order(
            pick(top_slope[1][0], low_slope_rest),
            pick(top_slope[1][1], other_core(low_slope_rest)),
        ),
    )
    grad_up = contract(saved, slope_grad, 0, 0).astype(jnp.bfloat16)
    low_blocks, grad_up = together(low_blocks, grad_up)
    bottom = (middle.astype(jnp.float32) + add_blocks(low_blocks)).astype(jnp.bfloat16)

    other = lax.ppermute(pick(bottom, middle), "section", [(0, 1), (1, 0)])
    grad_in = jnp.concatenate([pick(other, bottom), pick(middle, other)], axis=0)
    return grad_in[None], grad_up[None], grad_down[None]


def solution(mesh):
    fine = Mesh(mesh.devices.reshape(2, YLO, Z, X, CORES), AXES)
    wide, narrow = WIDE_AXES, ("x", "core")
    return jax.shard_map(
        body,
        mesh=fine,
        in_specs=(
            P("section", None, narrow),
            P(wide, narrow),
            P("section", narrow, wide),
            P("section", wide, narrow),
        ),
        out_specs=(
            P("section", wide, narrow),
            P("section", narrow, wide),
            P("section", wide, narrow),
        ),
        check_vma=False,
    )
```

```python
import jax
import jax.numpy as jnp
from jax import lax
from jax.sharding import Mesh, PartitionSpec as P

gelu_scale = 0.7978845608028654
cubic_term = 0.044715

X, CORES, YLO, Z = 4, 2, 2, 8
WIDE = YLO * Z
AXES = ("section", "ylo", "z", "x", "core")
WIDE_AXES = ("ylo", "z")
CROSS_AXES = ("section", "ylo")


def gelu_parts(pre_act):
    inner = jnp.tanh(gelu_scale * (pre_act + cubic_term * pre_act * pre_act * pre_act))
    act_value = 0.5 * pre_act * (1.0 + inner)
    slopes = 0.5 * (1.0 + inner) + 0.5 * pre_act * (1.0 - inner * inner) * gelu_scale * (
        1.0 + 3.0 * cubic_term * pre_act * pre_act
    )
    return (act_value, slopes)


def contract(first_op, second_op, first_dim, second_dim):
    return lax.dot_general(
        first_op,
        second_op,
        (((first_dim,), (second_dim,)), ((), ())),
        preferred_element_type=jnp.float32,
    )


def together(*values):
    return lax.optimization_barrier(values)


def other_core(block):
    return lax.ppermute(block, "core", [(0, 1), (1, 0)])


def to_upper(block):
    return lax.ppermute(block, CROSS_AXES, [(0, 3), (1, 2)])


def to_lower(block):
    return lax.ppermute(block, CROSS_AXES, [(3, 0), (2, 1)])


def halves(weight, dim):
    size = weight.shape[dim] // CORES
    core = lax.axis_index("core")
    return (
        lax.dynamic_slice_in_dim(weight, core * size, size, dim),
        lax.dynamic_slice_in_dim(weight, (1 - core) * size, size, dim),
    )


def in_order(mine, theirs):
    first = lax.axis_index("core") == 0
    return jnp.concatenate(
        [jnp.where(first, mine, theirs), jnp.where(first, theirs, mine)], axis=1
    )


def pair_sum(mine, theirs):
    return mine + other_core(theirs.astype(jnp.bfloat16)).astype(jnp.float32)


def spread_x(partial):
    rows, cols = partial.shape
    blocks = lax.all_to_all(
        partial.astype(jnp.bfloat16).reshape(X, rows // X, cols), "x", 0, 0, tiled=True
    )
    return jnp.sum(blocks.astype(jnp.float32), axis=0)


def gather_x(block):
    rows, cols = block.shape
    return lax.all_to_all(
        jnp.broadcast_to(block[None], (X, rows, cols)), "x", 0, 0, tiled=True
    ).reshape(X * rows, cols)


def step_x(block, distance):
    return lax.ppermute(block, "x", [(i, (i + distance) % X) for i in range(X)])


def spread_x_beside(partial):
    rows, cols = partial.shape
    x = lax.axis_index("x")
    blocks = partial.reshape(X, rows // X, cols)
    total = lax.dynamic_index_in_dim(blocks, x, 0, keepdims=False)
    sent = blocks.astype(jnp.bfloat16)
    for distance in (1, 3, 2):
        target = lax.rem(x + distance, X)
        block = lax.dynamic_index_in_dim(sent, target, 0, keepdims=False)
        total = total + step_x(block, distance).astype(jnp.float32)
    return total


def gather_x_beside(block):
    rows, cols = block.shape
    found = [block] + [step_x(block, X - distance) for distance in (1, 2, 3)]
    twice = jnp.stack(found + found[:-1])
    start = lax.rem(X - lax.axis_index("x"), X)
    return lax.dynamic_slice_in_dim(twice, start, X, 0).reshape(X * rows, cols)


def spread_wide(partial):
    rows, cols = partial.shape
    return lax.all_to_all(
        partial.reshape(WIDE, rows // WIDE, cols), WIDE_AXES, 0, 0, tiled=True
    )


def add_blocks(blocks):
    return jnp.sum(blocks.astype(jnp.float32), axis=0)


def gather_wide(block):
    rows, cols = block.shape
    return lax.all_to_all(
        jnp.broadcast_to(block[None], (WIDE, rows, cols)), WIDE_AXES, 0, 0, tiled=True
    ).reshape(WIDE * rows, cols)


def back_share(whole, down_halves):
    theirs = contract(whole, down_halves[1], 1, 1)
    mine = contract(whole, down_halves[0], 1, 1)
    return spread_x(pair_sum(mine, theirs))


def back_through_up(slope, up_halves):
    return (contract(slope[0], up_halves[0], 1, 1) + contract(slope[1], up_halves[1], 1, 1)).astype(
        jnp.bfloat16
    )


def body(saved_inputs, upstream, up_weight, down_weight):
    is_upper = lax.axis_index("section") == 1

    def pick(upper, lower):
        return jnp.where(is_upper, upper, lower)

    part = upstream.shape[0] // 2

    def part_of(block, index):
        rows, cols = block.shape
        split = block.reshape(rows // (2 * part), 2, part, cols)
        return split[:, index].reshape(rows // 2, cols)

    def both_parts(early, late):
        rows, cols = early.shape
        pair = [block.reshape(rows // part, part, cols) for block in (early, late)]
        return jnp.stack(pair, axis=1).reshape(2 * rows, cols)

    saved = saved_inputs[0]
    w_up, w_down = up_weight[0], down_weight[0]
    up_halves, down_halves = halves(w_up, 1), halves(w_down, 0)

    crossed = []
    for piece in (down_halves[1], down_halves[0], up_halves[0], up_halves[1]):
        crossed.append(to_upper(together(piece, *crossed[-1:])[0]))

    theirs = contract(saved, up_halves[1], 1, 0)
    mine = contract(saved, up_halves[0], 1, 0)
    pre = spread_x_beside(pair_sum(mine, theirs))
    act, slopes = gelu_parts(pre)
    act = act.astype(jnp.bfloat16)
    slopes = [part_of(slopes, c) for c in range(2)]
    gathered, act, *slopes = together(gather_wide(upstream), act, *slopes)

    share = back_share(gathered, down_halves)
    top_mine = [
        gather_x((part_of(share, c) * slopes[c]).astype(jnp.bfloat16)) for c in range(2)
    ]
    top_slope = [(block, other_core(block)) for block in top_mine]
    moved = to_lower(back_through_up(top_slope[0], up_halves))
    partial = pick(back_through_up(top_slope[1], up_halves), moved)
    partial, act, sent = together(partial, act, slopes[1].astype(jnp.bfloat16))
    blocks = spread_wide(partial)
    middle = (
        pick(upstream[part:], upstream[:part]).astype(jnp.float32) + add_blocks(blocks)
    ).astype(jnp.bfloat16)

    hidden = gather_x_beside(act)
    low, hidden, sent = together(gather_wide(middle), hidden, to_upper(sent))
    hidden = in_order(hidden, other_core(hidden))
    low_rest = to_lower(low)
    low_down = [pick(crossed[1], down_halves[0]), pick(crossed[0], down_halves[1])]
    low_share = back_share(low, low_down)
    incoming = pick(gathered, both_parts(low, low_rest))
    grad_down = contract(hidden, incoming, 0, 0).astype(jnp.bfloat16)
    low_mine = gather_x(
        (low_share * pick(sent.astype(jnp.float32), slopes[0])).astype(jnp.bfloat16)
    )
    low_mine, grad_down = together(low_mine, grad_down)
    low_slope = (low_mine, other_core(low_mine))
    low_slope_rest = to_lower(low_mine)
    low_up = [pick(crossed[2], up_halves[0]), pick(crossed[3], up_halves[1])]
    low_blocks = spread_wide(back_through_up(low_slope, low_up))
    slope_grad = both_parts(
        in_order(*[pick(u, l) for u, l in zip(top_slope[0], low_slope)]),
        in_order(
            pick(top_slope[1][0], low_slope_rest),
            pick(top_slope[1][1], other_core(low_slope_rest)),
        ),
    )
    grad_up = contract(saved, slope_grad, 0, 0).astype(jnp.bfloat16)
    low_blocks, grad_up = together(low_blocks, grad_up)
    bottom = (middle.astype(jnp.float32) + add_blocks(low_blocks)).astype(jnp.bfloat16)

    other = lax.ppermute(pick(bottom, middle), "section", [(0, 1), (1, 0)])
    grad_in = jnp.concatenate([pick(other, bottom), pick(middle, other)], axis=0)
    return grad_in[None], grad_up[None], grad_down[None]


def solution(mesh):
    fine = Mesh(mesh.devices.reshape(2, YLO, Z, X, CORES), AXES)
    wide, narrow = WIDE_AXES, ("x", "core")
    return jax.shard_map(
        body,
        mesh=fine,
        in_specs=(
            P("section", None, narrow),
            P(wide, narrow),
            P("section", narrow, wide),
            P("section", wide, narrow),
        ),
        out_specs=(
            P("section", wide, narrow),
            P("section", narrow, wide),
            P("section", wide, narrow),
        ),
        check_vma=False,
    )
```

```python
import jax
import jax.numpy as jnp
from jax import lax
from jax.sharding import Mesh, PartitionSpec as P

gelu_scale = 0.7978845608028654
cubic_term = 0.044715

X, CORES, YLO, Z = 4, 2, 2, 8
WIDE = YLO * Z
AXES = ("section", "ylo", "z", "x", "core")
WIDE_AXES = ("ylo", "z")
CROSS_AXES = ("section", "ylo")


def gelu_parts(pre_act):
    inner = jnp.tanh(gelu_scale * (pre_act + cubic_term * pre_act * pre_act * pre_act))
    act_value = 0.5 * pre_act * (1.0 + inner)
    slopes = 0.5 * (1.0 + inner) + 0.5 * pre_act * (1.0 - inner * inner) * gelu_scale * (
        1.0 + 3.0 * cubic_term * pre_act * pre_act
    )
    return (act_value, slopes)


def contract(first_op, second_op, first_dim, second_dim):
    return lax.dot_general(
        first_op,
        second_op,
        (((first_dim,), (second_dim,)), ((), ())),
        preferred_element_type=jnp.float32,
    )


def together(*values):
    return lax.optimization_barrier(values)


def other_core(block):
    return lax.ppermute(block, "core", [(0, 1), (1, 0)])


def to_upper(block):
    return lax.ppermute(block, CROSS_AXES, [(0, 3), (1, 2)])


def to_lower(block):
    return lax.ppermute(block, CROSS_AXES, [(3, 0), (2, 1)])


def halves(weight, dim):
    size = weight.shape[dim] // CORES
    core = lax.axis_index("core")
    return (
        lax.dynamic_slice_in_dim(weight, core * size, size, dim),
        lax.dynamic_slice_in_dim(weight, (1 - core) * size, size, dim),
    )


def in_order(mine, theirs):
    first = lax.axis_index("core") == 0
    return jnp.concatenate(
        [jnp.where(first, mine, theirs), jnp.where(first, theirs, mine)], axis=1
    )


def pair_sum(mine, theirs):
    return mine + other_core(theirs.astype(jnp.bfloat16)).astype(jnp.float32)


def spread_x(partial):
    rows, cols = partial.shape
    blocks = lax.all_to_all(
        partial.astype(jnp.bfloat16).reshape(X, rows // X, cols), "x", 0, 0, tiled=True
    )
    return jnp.sum(blocks.astype(jnp.float32), axis=0)


def gather_x(block):
    rows, cols = block.shape
    return lax.all_to_all(
        jnp.broadcast_to(block[None], (X, rows, cols)), "x", 0, 0, tiled=True
    ).reshape(X * rows, cols)


def step_x(block, distance):
    return lax.ppermute(block, "x", [(i, (i + distance) % X) for i in range(X)])


def spread_x_beside(partial):
    rows, cols = partial.shape
    x = lax.axis_index("x")
    blocks = partial.reshape(X, rows // X, cols)
    total = lax.dynamic_index_in_dim(blocks, x, 0, keepdims=False)
    sent = blocks.astype(jnp.bfloat16)
    for distance in (1, 3, 2):
        target = lax.rem(x + distance, X)
        block = lax.dynamic_index_in_dim(sent, target, 0, keepdims=False)
        total = total + step_x(block, distance).astype(jnp.float32)
    return total


def gather_x_beside(block):
    rows, cols = block.shape
    found = [block] + [step_x(block, distance) for distance in (1, 2, 3)]
    source = lax.broadcasted_iota(jnp.int32, (X, 1, 1), 0)
    passed = lax.rem(lax.axis_index("x") - source + X, X)
    placed = found[0][None]
    for distance in (1, 2, 3):
        placed = jnp.where(passed == distance, found[distance][None], placed)
    return placed.reshape(X * rows, cols)


def spread_wide(partial):
    rows, cols = partial.shape
    return lax.all_to_all(
        partial.reshape(WIDE, rows // WIDE, cols), WIDE_AXES, 0, 0, tiled=True
    )


def add_blocks(blocks):
    return jnp.sum(blocks.astype(jnp.float32), axis=0)


def gather_wide(block):
    rows, cols = block.shape
    return lax.all_to_all(
        jnp.broadcast_to(block[None], (WIDE, rows, cols)), WIDE_AXES, 0, 0, tiled=True
    ).reshape(WIDE * rows, cols)


def back_share(whole, down_halves):
    theirs = contract(whole, down_halves[1], 1, 1)
    mine = contract(whole, down_halves[0], 1, 1)
    return spread_x(pair_sum(mine, theirs))


def back_through_up(slope, up_halves):
    return (contract(slope[0], up_halves[0], 1, 1) + contract(slope[1], up_halves[1], 1, 1)).astype(
        jnp.bfloat16
    )


def body(saved_inputs, upstream, up_weight, down_weight):
    is_upper = lax.axis_index("section") == 1

    def pick(upper, lower):
        return jnp.where(is_upper, upper, lower)

    part = upstream.shape[0] // 2

    def part_of(block, index):
        rows, cols = block.shape
        split = block.reshape(rows // (2 * part), 2, part, cols)
        return split[:, index].reshape(rows // 2, cols)

    def both_parts(early, late):
        rows, cols = early.shape
        pair = [block.reshape(rows // part, part, cols) for block in (early, late)]
        return jnp.stack(pair, axis=1).reshape(2 * rows, cols)

    saved = saved_inputs[0]
    w_up, w_down = up_weight[0], down_weight[0]
    up_halves, down_halves = halves(w_up, 1), halves(w_down, 0)

    sent_down = to_upper(w_down)
    sent_up = []
    for piece in up_halves:
        sent_up.append(to_upper(together(piece, *(sent_up or [sent_down]))[0]))

    theirs = contract(saved, up_halves[1], 1, 0)
    mine = contract(saved, up_halves[0], 1, 0)
    pre = spread_x_beside(pair_sum(mine, theirs))
    act, slopes = gelu_parts(pre)
    act = act.astype(jnp.bfloat16)
    slopes = [part_of(slopes, c) for c in range(2)]
    gathered, act, *slopes = together(gather_wide(upstream), act, *slopes)

    share = back_share(gathered, down_halves)
    top_mine = [
        gather_x((part_of(share, c) * slopes[c]).astype(jnp.bfloat16)) for c in range(2)
    ]
    top_slope = [(block, other_core(block)) for block in top_mine]
    moved = to_lower(back_through_up(top_slope[0], up_halves))
    partial = pick(back_through_up(top_slope[1], up_halves), moved)
    partial, sent = together(partial, slopes[1].astype(jnp.bfloat16))
    blocks, act, sent_down = together(spread_wide(partial), act, sent_down)
    middle = (
        pick(upstream[part:], upstream[:part]).astype(jnp.float32) + add_blocks(blocks)
    ).astype(jnp.bfloat16)

    hidden = gather_x_beside(act)
    low, hidden, sent = together(gather_wide(middle), hidden, to_upper(sent))
    hidden = in_order(hidden, other_core(hidden))
    low_rest = to_lower(low)
    low_down = [pick(u, l) for u, l in zip(halves(sent_down, 0), down_halves)]
    low_share = back_share(low, low_down)
    incoming = pick(gathered, both_parts(low, low_rest))
    grad_down = contract(hidden, incoming, 0, 0).astype(jnp.bfloat16)
    low_mine = gather_x(
        (low_share * pick(sent.astype(jnp.float32), slopes[0])).astype(jnp.bfloat16)
    )
    low_mine, grad_down = together(low_mine, grad_down)
    low_slope = (low_mine, other_core(low_mine))
    low_slope_rest = to_lower(low_mine)
    low_up = [pick(u, l) for u, l in zip(sent_up, up_halves)]
    low_blocks = spread_wide(back_through_up(low_slope, low_up))
    slope_grad = both_parts(
        in_order(*[pick(u, l) for u, l in zip(top_slope[0], low_slope)]),
        in_order(
            pick(top_slope[1][0], low_slope_rest),
            pick(top_slope[1][1], other_core(low_slope_rest)),
        ),
    )
    grad_up = contract(saved, slope_grad, 0, 0).astype(jnp.bfloat16)
    low_blocks, grad_up = together(low_blocks, grad_up)
    bottom = (middle.astype(jnp.float32) + add_blocks(low_blocks)).astype(jnp.bfloat16)

    other = lax.ppermute(pick(bottom, middle), "section", [(0, 1), (1, 0)])
    grad_in = jnp.concatenate([pick(other, bottom), pick(middle, other)], axis=0)
    return grad_in[None], grad_up[None], grad_down[None]


def solution(mesh):
    fine = Mesh(mesh.devices.reshape(2, YLO, Z, X, CORES), AXES)
    wide, narrow = WIDE_AXES, ("x", "core")
    return jax.shard_map(
        body,
        mesh=fine,
        in_specs=(
            P("section", None, narrow),
            P(wide, narrow),
            P("section", narrow, wide),
            P("section", wide, narrow),
        ),
        out_specs=(
            P("section", wide, narrow),
            P("section", narrow, wide),
            P("section", wide, narrow),
        ),
        check_vma=False,
    )
```

```python
import jax
import jax.numpy as jnp
from jax import lax
from jax.sharding import Mesh, PartitionSpec as P

gelu_scale = 0.7978845608028654
cubic_term = 0.044715

X, CORES, YLO, Z = 4, 2, 2, 8
WIDE = YLO * Z
AXES = ("section", "ylo", "z", "x", "core")
WIDE_AXES = ("ylo", "z")
CROSS_AXES = ("section", "ylo")


def gelu_parts(pre_act):
    inner = jnp.tanh(gelu_scale * (pre_act + cubic_term * pre_act * pre_act * pre_act))
    act_value = 0.5 * pre_act * (1.0 + inner)
    slopes = 0.5 * (1.0 + inner) + 0.5 * pre_act * (1.0 - inner * inner) * gelu_scale * (
        1.0 + 3.0 * cubic_term * pre_act * pre_act
    )
    return (act_value, slopes)


def contract(first_op, second_op, first_dim, second_dim):
    return lax.dot_general(
        first_op,
        second_op,
        (((first_dim,), (second_dim,)), ((), ())),
        preferred_element_type=jnp.float32,
    )


def together(*values):
    return lax.optimization_barrier(values)


def other_core(block):
    return lax.ppermute(block, "core", [(0, 1), (1, 0)])


def to_upper(block):
    return lax.ppermute(block, CROSS_AXES, [(0, 3), (1, 2)])


def to_lower(block):
    return lax.ppermute(block, CROSS_AXES, [(3, 0), (2, 1)])


def halves(weight, dim):
    size = weight.shape[dim] // CORES
    core = lax.axis_index("core")
    return (
        lax.dynamic_slice_in_dim(weight, core * size, size, dim),
        lax.dynamic_slice_in_dim(weight, (1 - core) * size, size, dim),
    )


def in_order(mine, theirs):
    first = lax.axis_index("core") == 0
    return jnp.concatenate(
        [jnp.where(first, mine, theirs), jnp.where(first, theirs, mine)], axis=1
    )


def narrow_terms(mine, theirs):
    pair = mine + other_core(theirs.astype(jnp.bfloat16)).astype(jnp.float32)
    sent = pair.astype(jnp.bfloat16)
    routes = [[(i, (i + distance) % X) for i in range(X)] for distance in (1, 3, 2)]
    return [pair] + [lax.ppermute(sent, "x", route) for route in routes]


def add_terms(terms):
    return sum(term.astype(jnp.float32) for term in terms)


def spread_wide(partial):
    rows, cols = partial.shape
    return lax.all_to_all(
        partial.reshape(WIDE, rows // WIDE, cols), WIDE_AXES, 0, 0, tiled=True
    )


def add_blocks(blocks):
    return jnp.sum(blocks.astype(jnp.float32), axis=0)


def gather_wide(block):
    rows, cols = block.shape
    return lax.all_to_all(
        jnp.broadcast_to(block[None], (WIDE, rows, cols)), WIDE_AXES, 0, 0, tiled=True
    ).reshape(WIDE * rows, cols)


def back_total(whole, down_halves):
    theirs = contract(whole, down_halves[1], 1, 1)
    mine = contract(whole, down_halves[0], 1, 1)
    return add_terms(narrow_terms(mine, theirs))


def slope_of(total, slopes):
    mine = (total * slopes).astype(jnp.bfloat16)
    return mine, other_core(mine)


def back_through_up(slope, up_halves):
    return (contract(slope[0], up_halves[0], 1, 1) + contract(slope[1], up_halves[1], 1, 1)).astype(
        jnp.bfloat16
    )


def body(saved_inputs, upstream, up_weight, down_weight):
    is_upper = lax.axis_index("section") == 1

    def pick(upper, lower):
        return jnp.where(is_upper, upper, lower)

    def by_part(block):
        rows, cols = block.shape
        split = block.reshape(WIDE, 2, rows // (2 * WIDE), cols)
        return [split[:, c].reshape(rows // 2, cols) for c in range(2)]

    w_up, w_down = up_weight[0], down_weight[0]
    up_halves, down_halves = halves(w_up, 1), halves(w_down, 0)
    saved = by_part(saved_inputs[0])
    first, last = slice(0, saved[0].shape[0]), slice(saved[0].shape[0], None)

    sent_down = to_upper(w_down)

    theirs = jnp.concatenate([contract(rows, up_halves[1], 1, 0) for rows in saved], axis=0)
    mine = jnp.concatenate([contract(rows, up_halves[0], 1, 0) for rows in saved], axis=0)
    pre = narrow_terms(mine, theirs)
    gathered, pre[1], pre[2] = together(gather_wide(upstream), pre[1], pre[2])
    act, slopes = gelu_parts(add_terms(pre))
    act = act.astype(jnp.bfloat16)
    hidden = in_order(act, other_core(act))

    top = by_part(gathered)
    top_slope = slope_of(back_total(top[0], down_halves), slopes[first])
    moved = to_lower(back_through_up(top_slope, up_halves))
    late_slopes, _ = together(slopes[last], top_slope[0])
    top_slope_rest = slope_of(back_total(top[1], down_halves), late_slopes)
    partial = pick(back_through_up(top_slope_rest, up_halves), moved)
    half = w_up.shape[0] // 2
    sent_up = [to_upper(together(w_up[:half], sent_down)[0])]
    sent_up.append(to_upper(together(w_up[half:], sent_up[0])[0]))
    blocks, sent_down = together(spread_wide(partial), sent_down)
    part = upstream.shape[0] // 2
    middle = (
        pick(upstream[part:], upstream[:part]).astype(jnp.float32) + add_blocks(blocks)
    ).astype(jnp.bfloat16)

    low_down = pick(sent_down, w_down)
    lower_slopes = to_upper(slopes[last].astype(jnp.bfloat16))
    low, hidden, low_down, lower_slopes = together(
        gather_wide(middle), hidden, low_down, lower_slopes
    )
    lower_slopes = pick(lower_slopes.astype(jnp.float32), slopes[first])
    low_rest = to_lower(low)
    low_total = back_total(low, halves(low_down, 0))
    incoming = jnp.concatenate([pick(top[0], low), pick(top[1], low_rest)], axis=0)
    grad_down = contract(hidden, incoming, 0, 0).astype(jnp.bfloat16)
    low_total, grad_down, sent_up[1] = together(low_total, grad_down, sent_up[1])
    low_up = pick(jnp.concatenate(sent_up, axis=0), w_up)
    low_slope = slope_of(low_total, lower_slopes)
    low_slope_rest = to_lower(low_slope[0])
    low_blocks = spread_wide(back_through_up(low_slope, halves(low_up, 1)))
    slope_grad = jnp.concatenate(
        [
            in_order(*[pick(u, l) for u, l in zip(top_slope, low_slope)]),
            in_order(
                pick(top_slope_rest[0], low_slope_rest),
                pick(top_slope_rest[1], other_core(low_slope_rest)),
            ),
        ],
        axis=0,
    )
    grad_up = contract(jnp.concatenate(saved, axis=0), slope_grad, 0, 0).astype(jnp.bfloat16)
    low_blocks, grad_up = together(low_blocks, grad_up)
    bottom = (middle.astype(jnp.float32) + add_blocks(low_blocks)).astype(jnp.bfloat16)

    swap = [(0, 1), (1, 0)]
    upper_first = lax.ppermute(middle, "section", swap)
    lower_last = lax.ppermute(bottom, "section", swap)
    grad_in = jnp.concatenate([pick(upper_first, bottom), pick(middle, lower_last)], axis=0)
    return grad_in[None], grad_up[None], grad_down[None]


def solution(mesh):
    fine = Mesh(mesh.devices.reshape(2, YLO, Z, X, CORES), AXES)
    wide, narrow = WIDE_AXES, ("x", "core")
    return jax.shard_map(
        body,
        mesh=fine,
        in_specs=(
            P("section", None, narrow),
            P(wide, narrow),
            P("section", narrow, wide),
            P("section", wide, narrow),
        ),
        out_specs=(
            P("section", wide, narrow),
            P("section", narrow, wide),
            P("section", wide, narrow),
        ),
        check_vma=False,
    )
```

```python
import jax
import jax.numpy as jnp
from jax import lax
from jax.sharding import Mesh, PartitionSpec as P

gelu_scale = 0.7978845608028654
cubic_term = 0.044715

X, CORES, YLO, Z = 4, 2, 2, 8
WIDE = YLO * Z
AXES = ("section", "ylo", "z", "x", "core")
WIDE_AXES = ("ylo", "z")
CROSS_AXES = ("section", "ylo")


def gelu_parts(pre_act):
    inner = jnp.tanh(gelu_scale * (pre_act + cubic_term * pre_act * pre_act * pre_act))
    act_value = 0.5 * pre_act * (1.0 + inner)
    slopes = 0.5 * (1.0 + inner) + 0.5 * pre_act * (1.0 - inner * inner) * gelu_scale * (
        1.0 + 3.0 * cubic_term * pre_act * pre_act
    )
    return (act_value, slopes)


def contract(first_op, second_op, first_dim, second_dim):
    return lax.dot_general(
        first_op,
        second_op,
        (((first_dim,), (second_dim,)), ((), ())),
        preferred_element_type=jnp.float32,
    )


def together(*values):
    return lax.optimization_barrier(values)


def other_core(block):
    return lax.ppermute(block, "core", [(0, 1), (1, 0)])


def to_upper(block):
    return lax.ppermute(block, CROSS_AXES, [(0, 3), (1, 2)])


def to_lower(block):
    return lax.ppermute(block, CROSS_AXES, [(3, 0), (2, 1)])


def halves(weight, dim):
    size = weight.shape[dim] // CORES
    core = lax.axis_index("core")
    return (
        lax.dynamic_slice_in_dim(weight, core * size, size, dim),
        lax.dynamic_slice_in_dim(weight, (1 - core) * size, size, dim),
    )


def in_order(mine, theirs):
    first = lax.axis_index("core") == 0
    return jnp.concatenate(
        [jnp.where(first, mine, theirs), jnp.where(first, theirs, mine)], axis=1
    )


def pair_sum(mine, theirs):
    return mine + other_core(theirs.astype(jnp.bfloat16)).astype(jnp.float32)


def step_x(block, distance):
    return lax.ppermute(block, "x", [(i, (i + distance) % X) for i in range(X)])


def narrow_terms(mine, theirs):
    pair = pair_sum(mine, theirs)
    sent = pair.astype(jnp.bfloat16)
    return [pair] + [step_x(sent, distance) for distance in (1, 3, 2)]


def spread_x(partial):
    rows, cols = partial.shape
    x = lax.axis_index("x")
    blocks = partial.reshape(X, rows // X, cols)
    total = lax.dynamic_index_in_dim(blocks, x, 0, keepdims=False)
    sent = blocks.astype(jnp.bfloat16)
    for distance in (1, 3, 2):
        block = lax.dynamic_index_in_dim(sent, lax.rem(x + distance, X), 0, keepdims=False)
        total = total + step_x(block, distance).astype(jnp.float32)
    return total


def gather_x(block):
    rows, cols = block.shape
    found = [block] + [step_x(block, distance) for distance in (1, 2, 3)]
    source = lax.broadcasted_iota(jnp.int32, (X, 1, 1), 0)
    passed = lax.rem(lax.axis_index("x") - source + X, X)
    placed = found[0][None]
    for distance in (1, 2, 3):
        placed = jnp.where(passed == distance, found[distance][None], placed)
    return placed.reshape(X * rows, cols)


def add_terms(terms):
    return sum(term.astype(jnp.float32) for term in terms)


def spread_wide(partial):
    rows, cols = partial.shape
    return lax.all_to_all(
        partial.reshape(WIDE, rows // WIDE, cols), WIDE_AXES, 0, 0, tiled=True
    )


def add_blocks(blocks):
    return jnp.sum(blocks.astype(jnp.float32), axis=0)


def gather_wide(block):
    rows, cols = block.shape
    return lax.all_to_all(
        jnp.broadcast_to(block[None], (WIDE, rows, cols)), WIDE_AXES, 0, 0, tiled=True
    ).reshape(WIDE * rows, cols)


def back_total(whole, down_halves):
    theirs = contract(whole, down_halves[1], 1, 1)
    mine = contract(whole, down_halves[0], 1, 1)
    return add_terms(narrow_terms(mine, theirs))


def slope_of(total, slopes):
    mine = (total * slopes).astype(jnp.bfloat16)
    return mine, other_core(mine)


def back_through_up(slope, up_halves):
    return (contract(slope[0], up_halves[0], 1, 1) + contract(slope[1], up_halves[1], 1, 1)).astype(
        jnp.bfloat16
    )


def body(saved_inputs, upstream, up_weight, down_weight):
    is_upper = lax.axis_index("section") == 1

    def pick(upper, lower):
        return jnp.where(is_upper, upper, lower)

    def by_part(block):
        rows, cols = block.shape
        split = block.reshape(WIDE, 2, rows // (2 * WIDE), cols)
        return [split[:, c].reshape(rows // 2, cols) for c in range(2)]

    w_up, w_down = up_weight[0], down_weight[0]
    up_halves, down_halves = halves(w_up, 1), halves(w_down, 0)
    saved = by_part(saved_inputs[0])
    first, last = slice(0, saved[0].shape[0]), slice(saved[0].shape[0], None)

    sent_down = to_upper(w_down)

    theirs = jnp.concatenate([contract(rows, up_halves[1], 1, 0) for rows in saved], axis=0)
    mine = jnp.concatenate([contract(rows, up_halves[0], 1, 0) for rows in saved], axis=0)
    act, slopes = gelu_parts(spread_x(pair_sum(mine, theirs)))
    act = act.astype(jnp.bfloat16)
    slopes = gather_x(slopes.astype(jnp.bfloat16))
    gathered, act, slopes = together(gather_wide(upstream), act, slopes)

    top = by_part(gathered)
    top_slope = slope_of(back_total(top[0], down_halves), slopes[first])
    moved = to_lower(back_through_up(top_slope, up_halves))
    late_slopes, _ = together(slopes[last], top_slope[0])
    top_slope_rest = slope_of(back_total(top[1], down_halves), late_slopes)
    partial = pick(back_through_up(top_slope_rest, up_halves), moved)
    half = w_up.shape[0] // 2
    sent_up = [to_upper(together(w_up[:half], sent_down)[0])]
    sent_up.append(to_upper(together(w_up[half:], sent_up[0])[0]))
    partial, act = together(partial, act)
    blocks, sent_down = together(spread_wide(partial), sent_down)
    part = upstream.shape[0] // 2
    middle = (
        pick(upstream[part:], upstream[:part]).astype(jnp.float32) + add_blocks(blocks)
    ).astype(jnp.bfloat16)

    low_down = pick(sent_down, w_down)
    lower_slopes = to_upper(slopes[last])
    hidden = gather_x(act)
    hidden = in_order(hidden, other_core(hidden))
    low, hidden, low_down, lower_slopes = together(
        gather_wide(middle), hidden, low_down, lower_slopes
    )
    lower_slopes = pick(lower_slopes, slopes[first])
    low_rest = to_lower(low)
    low_total = back_total(low, halves(low_down, 0))
    incoming = jnp.concatenate([pick(top[0], low), pick(top[1], low_rest)], axis=0)
    grad_down = contract(hidden, incoming, 0, 0).astype(jnp.bfloat16)
    low_total, grad_down, sent_up[1] = together(low_total, grad_down, sent_up[1])
    low_up = pick(jnp.concatenate(sent_up, axis=0), w_up)
    low_slope = slope_of(low_total, lower_slopes)
    low_slope_rest = to_lower(low_slope[0])
    low_blocks = spread_wide(back_through_up(low_slope, halves(low_up, 1)))
    slope_grad = jnp.concatenate(
        [
            in_order(*[pick(u, l) for u, l in zip(top_slope, low_slope)]),
            in_order(
                pick(top_slope_rest[0], low_slope_rest),
                pick(top_slope_rest[1], other_core(low_slope_rest)),
            ),
        ],
        axis=0,
    )
    grad_up = contract(jnp.concatenate(saved, axis=0), slope_grad, 0, 0).astype(jnp.bfloat16)
    low_blocks, grad_up = together(low_blocks, grad_up)
    bottom = (middle.astype(jnp.float32) + add_blocks(low_blocks)).astype(jnp.bfloat16)

    swap = [(0, 1), (1, 0)]
    upper_first = lax.ppermute(middle, "section", swap)
    lower_last = lax.ppermute(bottom, "section", swap)
    grad_in = jnp.concatenate([pick(upper_first, bottom), pick(middle, lower_last)], axis=0)
    return grad_in[None], grad_up[None], grad_down[None]


def solution(mesh):
    fine = Mesh(mesh.devices.reshape(2, YLO, Z, X, CORES), AXES)
    wide, narrow = WIDE_AXES, ("x", "core")
    return jax.shard_map(
        body,
        mesh=fine,
        in_specs=(
            P("section", None, narrow),
            P(wide, narrow),
            P("section", narrow, wide),
            P("section", wide, narrow),
        ),
        out_specs=(
            P("section", wide, narrow),
            P("section", narrow, wide),
            P("section", wide, narrow),
        ),
        check_vma=False,
    )
```

```python
import jax
import jax.numpy as jnp
from jax import lax
from jax.sharding import Mesh, PartitionSpec as P

gelu_scale = 0.7978845608028654
cubic_term = 0.044715

X, CORES, YLO, Z = 4, 2, 2, 8
WIDE = YLO * Z
AXES = ("section", "ylo", "z", "x", "core")
WIDE_AXES = ("ylo", "z")
CROSS_AXES = ("section", "ylo")


def gelu_parts(pre_act):
    inner = jnp.tanh(gelu_scale * (pre_act + cubic_term * pre_act * pre_act * pre_act))
    act_value = 0.5 * pre_act * (1.0 + inner)
    slopes = 0.5 * (1.0 + inner) + 0.5 * pre_act * (1.0 - inner * inner) * gelu_scale * (
        1.0 + 3.0 * cubic_term * pre_act * pre_act
    )
    return (act_value, slopes)


def contract(first_op, second_op, first_dim, second_dim):
    return lax.dot_general(
        first_op,
        second_op,
        (((first_dim,), (second_dim,)), ((), ())),
        preferred_element_type=jnp.float32,
    )


def together(*values):
    return lax.optimization_barrier(values)


def other_core(block):
    return lax.ppermute(block, "core", [(0, 1), (1, 0)])


def to_upper(block):
    return lax.ppermute(block, CROSS_AXES, [(0, 3), (1, 2)])


def to_lower(block):
    return lax.ppermute(block, CROSS_AXES, [(3, 0), (2, 1)])


def halves(weight, dim):
    size = weight.shape[dim] // CORES
    core = lax.axis_index("core")
    return (
        lax.dynamic_slice_in_dim(weight, core * size, size, dim),
        lax.dynamic_slice_in_dim(weight, (1 - core) * size, size, dim),
    )


def in_order(mine, theirs):
    first = lax.axis_index("core") == 0
    return jnp.concatenate(
        [jnp.where(first, mine, theirs), jnp.where(first, theirs, mine)], axis=1
    )


def pair_sum(mine, theirs):
    return mine + other_core(theirs.astype(jnp.bfloat16)).astype(jnp.float32)


def step_x(block, distance):
    return lax.ppermute(block, "x", [(i, (i + distance) % X) for i in range(X)])


def narrow_terms(mine, theirs):
    pair = pair_sum(mine, theirs)
    sent = pair.astype(jnp.bfloat16)
    return [pair] + [step_x(sent, distance) for distance in (1, 3, 2)]


def spread_x(partial):
    rows, cols = partial.shape
    x = lax.axis_index("x")
    blocks = partial.reshape(X, rows // X, cols)
    total = lax.dynamic_index_in_dim(blocks, x, 0, keepdims=False)
    sent = blocks.astype(jnp.bfloat16)
    for distance in (1, 3, 2):
        block = lax.dynamic_index_in_dim(sent, lax.rem(x + distance, X), 0, keepdims=False)
        total = total + step_x(block, distance).astype(jnp.float32)
    return total


def gather_x(block):
    rows, cols = block.shape
    found = [block] + [step_x(block, distance) for distance in (1, 2, 3)]
    source = lax.broadcasted_iota(jnp.int32, (X, 1, 1), 0)
    passed = lax.rem(lax.axis_index("x") - source + X, X)
    placed = found[0][None]
    for distance in (1, 2, 3):
        placed = jnp.where(passed == distance, found[distance][None], placed)
    return placed.reshape(X * rows, cols)


def add_terms(terms):
    return sum(term.astype(jnp.float32) for term in terms)


def spread_wide(partial):
    rows, cols = partial.shape
    return lax.all_to_all(
        partial.reshape(WIDE, rows // WIDE, cols), WIDE_AXES, 0, 0, tiled=True
    )


def add_blocks(blocks):
    return jnp.sum(blocks.astype(jnp.float32), axis=0)


def gather_wide(block):
    rows, cols = block.shape
    return lax.all_to_all(
        jnp.broadcast_to(block[None], (WIDE, rows, cols)), WIDE_AXES, 0, 0, tiled=True
    ).reshape(WIDE * rows, cols)


def back_total(whole, down_halves):
    theirs = contract(whole, down_halves[1], 1, 1)
    mine = contract(whole, down_halves[0], 1, 1)
    return add_terms(narrow_terms(mine, theirs))


def slope_of(total, slopes):
    mine = (total * slopes).astype(jnp.bfloat16)
    return mine, other_core(mine)


def back_through_up(slope, up_halves):
    return (contract(slope[0], up_halves[0], 1, 1) + contract(slope[1], up_halves[1], 1, 1)).astype(
        jnp.bfloat16
    )


def body(saved_inputs, upstream, up_weight, down_weight):
    is_upper = lax.axis_index("section") == 1

    def pick(upper, lower):
        return jnp.where(is_upper, upper, lower)

    def by_part(block):
        rows, cols = block.shape
        split = block.reshape(WIDE, 2, rows // (2 * WIDE), cols)
        return [split[:, c].reshape(rows // 2, cols) for c in range(2)]

    w_up, w_down = up_weight[0], down_weight[0]
    up_halves, down_halves = halves(w_up, 1), halves(w_down, 0)
    saved = by_part(saved_inputs[0])
    first, last = slice(0, saved[0].shape[0]), slice(saved[0].shape[0], None)

    sent_down = to_upper(w_down)

    theirs = jnp.concatenate([contract(rows, up_halves[1], 1, 0) for rows in saved], axis=0)
    mine = jnp.concatenate([contract(rows, up_halves[0], 1, 0) for rows in saved], axis=0)
    act, slopes = gelu_parts(spread_x(pair_sum(mine, theirs)))
    act = act.astype(jnp.bfloat16)
    slopes = gather_x(slopes.astype(jnp.bfloat16))
    gathered, act = together(gather_wide(upstream), act)

    top = by_part(gathered)
    theirs = contract(top[0], down_halves[1], 1, 1)
    mine = contract(top[0], down_halves[0], 1, 1)
    mine, slopes = together(mine, slopes)
    top_slope = slope_of(add_terms(narrow_terms(mine, theirs)), slopes[first])
    moved = to_lower(back_through_up(top_slope, up_halves))
    late_slopes, _ = together(slopes[last], top_slope[0])
    top_slope_rest = slope_of(back_total(top[1], down_halves), late_slopes)
    partial = pick(back_through_up(top_slope_rest, up_halves), moved)
    half = w_up.shape[0] // 2
    sent_up = [to_upper(together(w_up[:half], sent_down)[0])]
    sent_up.append(to_upper(together(w_up[half:], sent_up[0])[0]))
    partial, act = together(partial, act)
    blocks, low_down, lower_slopes = together(
        spread_wide(partial), pick(sent_down, w_down), to_upper(slopes[last])
    )
    part = upstream.shape[0] // 2
    middle = (
        pick(upstream[part:], upstream[:part]).astype(jnp.float32) + add_blocks(blocks)
    ).astype(jnp.bfloat16)

    hidden = gather_x(in_order(act, other_core(act)))
    low, hidden = together(gather_wide(middle), hidden)
    lower_slopes = pick(lower_slopes, slopes[first])
    low_rest = to_lower(low)
    low_total = back_total(low, halves(low_down, 0))
    incoming = jnp.concatenate([pick(top[0], low), pick(top[1], low_rest)], axis=0)
    incoming, sent_up[1] = together(incoming, sent_up[1])
    grad_down = contract(hidden, incoming, 0, 0).astype(jnp.bfloat16)
    low_up = pick(jnp.concatenate(sent_up, axis=0), w_up)
    low_total, grad_down, low_up = together(low_total, grad_down, low_up)
    low_slope = slope_of(low_total, lower_slopes)
    low_slope_rest = to_lower(low_slope[0])
    low_blocks = spread_wide(back_through_up(low_slope, halves(low_up, 1)))
    slope_grad = jnp.concatenate(
        [
            in_order(*[pick(u, l) for u, l in zip(top_slope, low_slope)]),
            in_order(
                pick(top_slope_rest[0], low_slope_rest),
                pick(top_slope_rest[1], other_core(low_slope_rest)),
            ),
        ],
        axis=0,
    )
    grad_up = contract(jnp.concatenate(saved, axis=0), slope_grad, 0, 0).astype(jnp.bfloat16)
    low_blocks, grad_up = together(low_blocks, grad_up)
    bottom = (middle.astype(jnp.float32) + add_blocks(low_blocks)).astype(jnp.bfloat16)

    swap = [(0, 1), (1, 0)]
    upper_first = lax.ppermute(middle, "section", swap)
    lower_last = lax.ppermute(bottom, "section", swap)
    grad_in = jnp.concatenate([pick(upper_first, bottom), pick(middle, lower_last)], axis=0)
    return grad_in[None], grad_up[None], grad_down[None]


def solution(mesh):
    fine = Mesh(mesh.devices.reshape(2, YLO, Z, X, CORES), AXES)
    wide, narrow = WIDE_AXES, ("x", "core")
    return jax.shard_map(
        body,
        mesh=fine,
        in_specs=(
            P("section", None, narrow),
            P(wide, narrow),
            P("section", narrow, wide),
            P("section", wide, narrow),
        ),
        out_specs=(
            P("section", wide, narrow),
            P("section", narrow, wide),
            P("section", wide, narrow),
        ),
        check_vma=False,
    )
```

```python
import jax
import jax.numpy as jnp
from jax import lax
from jax.sharding import Mesh, PartitionSpec as P

gelu_scale = 0.7978845608028654
cubic_term = 0.044715

X, CORES, YLO, Z = 4, 2, 2, 8
WIDE = YLO * Z
AXES = ("section", "ylo", "z", "x", "core")
WIDE_AXES = ("ylo", "z")
CROSS_AXES = ("section", "ylo")


def gelu_parts(pre_act):
    inner = jnp.tanh(gelu_scale * (pre_act + cubic_term * pre_act * pre_act * pre_act))
    act_value = 0.5 * pre_act * (1.0 + inner)
    slopes = 0.5 * (1.0 + inner) + 0.5 * pre_act * (1.0 - inner * inner) * gelu_scale * (
        1.0 + 3.0 * cubic_term * pre_act * pre_act
    )
    return (act_value, slopes)


def contract(first_op, second_op, first_dim, second_dim):
    return lax.dot_general(
        first_op,
        second_op,
        (((first_dim,), (second_dim,)), ((), ())),
        preferred_element_type=jnp.float32,
    )


def together(*values):
    return lax.optimization_barrier(values)


def other_core(block):
    return lax.ppermute(block, "core", [(0, 1), (1, 0)])


def to_upper(block):
    return lax.ppermute(block, CROSS_AXES, [(0, 3), (1, 2)])


def to_lower(block):
    return lax.ppermute(block, CROSS_AXES, [(3, 0), (2, 1)])


def halves(weight, dim):
    size = weight.shape[dim] // CORES
    core = lax.axis_index("core")
    return (
        lax.dynamic_slice_in_dim(weight, core * size, size, dim),
        lax.dynamic_slice_in_dim(weight, (1 - core) * size, size, dim),
    )


def in_order(mine, theirs):
    first = lax.axis_index("core") == 0
    return jnp.concatenate(
        [jnp.where(first, mine, theirs), jnp.where(first, theirs, mine)], axis=1
    )


def pair_sum(mine, theirs):
    return mine + other_core(theirs.astype(jnp.bfloat16)).astype(jnp.float32)


def step_x(block, distance):
    return lax.ppermute(block, "x", [(i, (i + distance) % X) for i in range(X)])


def narrow_terms(pair):
    sent = pair.astype(jnp.bfloat16)
    return [pair] + [step_x(sent, distance) for distance in (1, 3, 2)]


def spread_x(partial):
    rows, cols = partial.shape
    x = lax.axis_index("x")
    blocks = partial.reshape(X, rows // X, cols)
    total = lax.dynamic_index_in_dim(blocks, x, 0, keepdims=False)
    sent = blocks.astype(jnp.bfloat16)
    for distance in (1, 3, 2):
        block = lax.dynamic_index_in_dim(sent, lax.rem(x + distance, X), 0, keepdims=False)
        total = total + step_x(block, distance).astype(jnp.float32)
    return total


def send_x(block):
    return [block] + [step_x(block, distance) for distance in (1, 2, 3)]


def place_x(found):
    rows, cols = found[0].shape
    source = lax.broadcasted_iota(jnp.int32, (X, 1, 1), 0)
    passed = lax.rem(lax.axis_index("x") - source + X, X)
    placed = found[0][None]
    for distance in (1, 2, 3):
        placed = jnp.where(passed == distance, found[distance][None], placed)
    return placed.reshape(X * rows, cols)


def add_terms(terms):
    return sum(term.astype(jnp.float32) for term in terms)


def spread_wide(partial):
    rows, cols = partial.shape
    return lax.all_to_all(
        partial.reshape(WIDE, rows // WIDE, cols), WIDE_AXES, 0, 0, tiled=True
    )


def add_blocks(blocks):
    return jnp.sum(blocks.astype(jnp.float32), axis=0)


def gather_wide(block):
    rows, cols = block.shape
    return lax.all_to_all(
        jnp.broadcast_to(block[None], (WIDE, rows, cols)), WIDE_AXES, 0, 0, tiled=True
    ).reshape(WIDE * rows, cols)


def back_total(whole, down_halves):
    theirs = contract(whole, down_halves[1], 1, 1)
    mine = contract(whole, down_halves[0], 1, 1)
    return add_terms(narrow_terms(pair_sum(mine, theirs)))


def slope_of(total, slopes):
    mine = (total * slopes).astype(jnp.bfloat16)
    return mine, other_core(mine)


def back_through_up(slope, up_halves):
    return (contract(slope[0], up_halves[0], 1, 1) + contract(slope[1], up_halves[1], 1, 1)).astype(
        jnp.bfloat16
    )


def body(saved_inputs, upstream, up_weight, down_weight):
    is_upper = lax.axis_index("section") == 1

    def pick(upper, lower):
        return jnp.where(is_upper, upper, lower)

    def by_part(block):
        rows, cols = block.shape
        split = block.reshape(WIDE, 2, rows // (2 * WIDE), cols)
        return [split[:, c].reshape(rows // 2, cols) for c in range(2)]

    w_up, w_down = up_weight[0], down_weight[0]
    up_halves, down_halves = halves(w_up, 1), halves(w_down, 0)
    saved = by_part(saved_inputs[0])
    first, last = slice(0, saved[0].shape[0]), slice(saved[0].shape[0], None)

    sent_down = to_upper(w_down)

    theirs = jnp.concatenate([contract(rows, up_halves[1], 1, 0) for rows in saved], axis=0)
    mine = jnp.concatenate([contract(rows, up_halves[0], 1, 0) for rows in saved], axis=0)
    act, slopes = gelu_parts(spread_x(pair_sum(mine, theirs)))
    act = act.astype(jnp.bfloat16)
    slopes = place_x(send_x(slopes.astype(jnp.bfloat16)))
    gathered, act = together(gather_wide(upstream), act)

    top = by_part(gathered)
    theirs = contract(top[0], down_halves[1], 1, 1)
    mine = contract(top[0], down_halves[0], 1, 1)
    mine, slopes = together(mine, slopes)
    top_slope = slope_of(add_terms(narrow_terms(pair_sum(mine, theirs))), slopes[first])
    moved = to_lower(back_through_up(top_slope, up_halves))
    late_slopes, _ = together(slopes[last], top_slope[0])
    top_slope_rest = slope_of(back_total(top[1], down_halves), late_slopes)
    partial = pick(back_through_up(top_slope_rest, up_halves), moved)
    half = w_up.shape[0] // 2
    sent_up = [to_upper(together(w_up[:half], sent_down)[0])]
    sent_up.append(to_upper(together(w_up[half:], sent_up[0])[0]))
    partial, act = together(partial, act)
    own = in_order(act, other_core(act))
    blocks, lower_slopes, _ = together(spread_wide(partial), to_upper(slopes[last]), own)
    low_down = pick(sent_down, w_down)
    part = upstream.shape[0] // 2
    middle = (
        pick(upstream[part:], upstream[:part]).astype(jnp.float32) + add_blocks(blocks)
    ).astype(jnp.bfloat16)

    hidden = send_x(own)
    low = gather_wide(middle)
    lower_slopes = pick(lower_slopes, slopes[first])
    low_rest = to_lower(low)
    low_halves = halves(low_down, 0)
    theirs = contract(low, low_halves[1], 1, 1)
    mine = contract(low, low_halves[0], 1, 1)
    hidden[0], theirs = together(hidden[0], theirs)
    pair, hidden = together(pair_sum(mine, theirs), place_x(hidden))
    low_total = add_terms(narrow_terms(pair))
    incoming = jnp.concatenate([pick(top[0], low), pick(top[1], low_rest)], axis=0)
    incoming, sent_up[1] = together(incoming, sent_up[1])
    grad_down = contract(hidden, incoming, 0, 0).astype(jnp.bfloat16)
    low_up = pick(jnp.concatenate(sent_up, axis=0), w_up)
    low_total, grad_down, low_up = together(low_total, grad_down, low_up)
    low_slope = slope_of(low_total, lower_slopes)
    low_slope_rest = to_lower(low_slope[0])
    low_blocks = spread_wide(back_through_up(low_slope, halves(low_up, 1)))
    slope_grad = jnp.concatenate(
        [
            in_order(*[pick(u, l) for u, l in zip(top_slope, low_slope)]),
            in_order(
                pick(top_slope_rest[0], low_slope_rest),
                pick(top_slope_rest[1], other_core(low_slope_rest)),
            ),
        ],
        axis=0,
    )
    grad_up = contract(jnp.concatenate(saved, axis=0), slope_grad, 0, 0).astype(jnp.bfloat16)
    low_blocks, grad_up = together(low_blocks, grad_up)
    bottom = (middle.astype(jnp.float32) + add_blocks(low_blocks)).astype(jnp.bfloat16)

    swap = [(0, 1), (1, 0)]
    upper_first = lax.ppermute(middle, "section", swap)
    lower_last = lax.ppermute(bottom, "section", swap)
    grad_in = jnp.concatenate([pick(upper_first, bottom), pick(middle, lower_last)], axis=0)
    return grad_in[None], grad_up[None], grad_down[None]


def solution(mesh):
    fine = Mesh(mesh.devices.reshape(2, YLO, Z, X, CORES), AXES)
    wide, narrow = WIDE_AXES, ("x", "core")
    return jax.shard_map(
        body,
        mesh=fine,
        in_specs=(
            P("section", None, narrow),
            P(wide, narrow),
            P("section", narrow, wide),
            P("section", wide, narrow),
        ),
        out_specs=(
            P("section", wide, narrow),
            P("section", narrow, wide),
            P("section", wide, narrow),
        ),
        check_vma=False,
    )
```

```python
import jax
import jax.numpy as jnp
from jax import lax
from jax.sharding import Mesh, PartitionSpec as P

gelu_scale = 0.7978845608028654
cubic_term = 0.044715

X, CORES, YLO, Z = 4, 2, 2, 8
WIDE = YLO * Z
AXES = ("section", "ylo", "z", "x", "core")
WIDE_AXES = ("ylo", "z")
CROSS_AXES = ("section", "ylo")


def gelu_parts(pre_act):
    inner = jnp.tanh(gelu_scale * (pre_act + cubic_term * pre_act * pre_act * pre_act))
    act_value = 0.5 * pre_act * (1.0 + inner)
    slopes = 0.5 * (1.0 + inner) + 0.5 * pre_act * (1.0 - inner * inner) * gelu_scale * (
        1.0 + 3.0 * cubic_term * pre_act * pre_act
    )
    return (act_value, slopes)


def contract(first_op, second_op, first_dim, second_dim):
    return lax.dot_general(
        first_op,
        second_op,
        (((first_dim,), (second_dim,)), ((), ())),
        preferred_element_type=jnp.float32,
    )


def together(*values):
    return lax.optimization_barrier(values)


def other_core(block):
    return lax.ppermute(block, "core", [(0, 1), (1, 0)])


def to_upper(block):
    return lax.ppermute(block, CROSS_AXES, [(0, 3), (1, 2)])


def to_lower(block):
    return lax.ppermute(block, CROSS_AXES, [(3, 0), (2, 1)])


def halves(weight, dim):
    size = weight.shape[dim] // CORES
    core = lax.axis_index("core")
    return (
        lax.dynamic_slice_in_dim(weight, core * size, size, dim),
        lax.dynamic_slice_in_dim(weight, (1 - core) * size, size, dim),
    )


def in_order(mine, theirs):
    first = lax.axis_index("core") == 0
    return jnp.concatenate(
        [jnp.where(first, mine, theirs), jnp.where(first, theirs, mine)], axis=1
    )


def pair_sum(mine, theirs):
    return mine + other_core(theirs.astype(jnp.bfloat16)).astype(jnp.float32)


def step_x(block, distance):
    return lax.ppermute(block, "x", [(i, (i + distance) % X) for i in range(X)])


def narrow_terms(pair):
    sent = pair.astype(jnp.bfloat16)
    return [pair] + [step_x(sent, distance) for distance in (1, 3, 2)]


def spread_x(partial):
    rows, cols = partial.shape
    x = lax.axis_index("x")
    blocks = partial.reshape(X, rows // X, cols)
    total = lax.dynamic_index_in_dim(blocks, x, 0, keepdims=False)
    sent = blocks.astype(jnp.bfloat16)
    for distance in (1, 3, 2):
        block = lax.dynamic_index_in_dim(sent, lax.rem(x + distance, X), 0, keepdims=False)
        total = total + step_x(block, distance).astype(jnp.float32)
    return total


def send_x(block):
    return [block] + [step_x(block, distance) for distance in (1, 2, 3)]


def place_x(found):
    rows, cols = found[0].shape
    source = lax.broadcasted_iota(jnp.int32, (X, 1, 1), 0)
    passed = lax.rem(lax.axis_index("x") - source + X, X)
    placed = found[0][None]
    for distance in (1, 2, 3):
        placed = jnp.where(passed == distance, found[distance][None], placed)
    return placed.reshape(X * rows, cols)


def add_terms(terms):
    return sum(term.astype(jnp.float32) for term in terms)


def spread_wide(partial):
    rows, cols = partial.shape
    return lax.all_to_all(
        partial.reshape(WIDE, rows // WIDE, cols), WIDE_AXES, 0, 0, tiled=True
    )


def add_blocks(blocks):
    return jnp.sum(blocks.astype(jnp.float32), axis=0)


def gather_wide(block):
    rows, cols = block.shape
    return lax.all_to_all(
        jnp.broadcast_to(block[None], (WIDE, rows, cols)), WIDE_AXES, 0, 0, tiled=True
    ).reshape(WIDE * rows, cols)


def back_total(whole, down_halves):
    theirs = contract(whole, down_halves[1], 1, 1)
    mine = contract(whole, down_halves[0], 1, 1)
    return add_terms(narrow_terms(pair_sum(mine, theirs)))


def slope_of(total, slopes):
    mine = (total * slopes).astype(jnp.bfloat16)
    return mine, other_core(mine)


def back_through_up(slope, up_halves):
    return (contract(slope[0], up_halves[0], 1, 1) + contract(slope[1], up_halves[1], 1, 1)).astype(
        jnp.bfloat16
    )


def body(saved_inputs, upstream, up_weight, down_weight):
    is_upper = lax.axis_index("section") == 1

    def pick(upper, lower):
        return jnp.where(is_upper, upper, lower)

    def by_part(block):
        rows, cols = block.shape
        split = block.reshape(WIDE, 2, rows // (2 * WIDE), cols)
        return [split[:, c].reshape(rows // 2, cols) for c in range(2)]

    w_up, w_down = up_weight[0], down_weight[0]
    up_halves, down_halves = halves(w_up, 1), halves(w_down, 0)
    saved = by_part(saved_inputs[0])
    first, last = slice(0, saved[0].shape[0]), slice(saved[0].shape[0], None)

    sent_down = to_upper(w_down)

    theirs = jnp.concatenate([contract(rows, up_halves[1], 1, 0) for rows in saved], axis=0)
    mine = jnp.concatenate([contract(rows, up_halves[0], 1, 0) for rows in saved], axis=0)
    act, slopes = gelu_parts(spread_x(pair_sum(mine, theirs)))
    act = act.astype(jnp.bfloat16)
    slopes = place_x(send_x(slopes.astype(jnp.bfloat16)))
    gathered, act = together(gather_wide(upstream), act)

    top = by_part(gathered)
    theirs = contract(top[0], down_halves[1], 1, 1)
    mine = contract(top[0], down_halves[0], 1, 1)
    mine, slopes = together(mine, slopes)
    top_slope = slope_of(add_terms(narrow_terms(pair_sum(mine, theirs))), slopes[first])
    moved = to_lower(back_through_up(top_slope, up_halves))
    late_slopes, _ = together(slopes[last], top_slope[0])
    top_slope_rest = slope_of(back_total(top[1], down_halves), late_slopes)
    partial = pick(back_through_up(top_slope_rest, up_halves), moved)
    half = w_up.shape[0] // 2
    sent_up = [to_upper(together(w_up[:half], sent_down)[0])]
    sent_up.append(to_upper(together(w_up[half:], sent_up[0])[0]))
    partial, act = together(partial, act)
    own = in_order(act, other_core(act))
    blocks, lower_slopes, _ = together(spread_wide(partial), to_upper(slopes[last]), own)
    low_down = pick(sent_down, w_down)
    part = upstream.shape[0] // 2
    middle = (
        pick(upstream[part:], upstream[:part]).astype(jnp.float32) + add_blocks(blocks)
    ).astype(jnp.bfloat16)

    hidden = send_x(own)
    low = gather_wide(middle)
    lower_slopes = pick(lower_slopes, slopes[first])
    low_rest = to_lower(low)
    low_halves = halves(low_down, 0)
    theirs = contract(low, low_halves[1], 1, 1)
    mine = contract(low, low_halves[0], 1, 1)
    hidden[0], theirs = together(hidden[0], theirs)
    pair, hidden = together(pair_sum(mine, theirs), place_x(hidden))
    low_total = add_terms(narrow_terms(pair))
    incoming = jnp.concatenate([pick(top[0], low), pick(top[1], low_rest)], axis=0)
    grad_down = contract(hidden, incoming, 0, 0).astype(jnp.bfloat16)
    low_total, grad_down, sent_up[1] = together(low_total, grad_down, sent_up[1])
    low_up = pick(jnp.concatenate(sent_up, axis=0), w_up)
    low_slope = slope_of(low_total, lower_slopes)
    low_slope_rest = to_lower(low_slope[0])
    low_blocks = spread_wide(back_through_up(low_slope, halves(low_up, 1)))
    slope_grad = jnp.concatenate(
        [
            in_order(*[pick(u, l) for u, l in zip(top_slope, low_slope)]),
            in_order(
                pick(top_slope_rest[0], low_slope_rest),
                pick(top_slope_rest[1], other_core(low_slope_rest)),
            ),
        ],
        axis=0,
    )
    grad_up = contract(jnp.concatenate(saved, axis=0), slope_grad, 0, 0).astype(jnp.bfloat16)
    low_blocks, grad_up = together(low_blocks, grad_up)
    bottom = (middle.astype(jnp.float32) + add_blocks(low_blocks)).astype(jnp.bfloat16)

    swap = [(0, 1), (1, 0)]
    upper_first = lax.ppermute(middle, "section", swap)
    lower_last = lax.ppermute(bottom, "section", swap)
    grad_in = jnp.concatenate([pick(upper_first, bottom), pick(middle, lower_last)], axis=0)
    return grad_in[None], grad_up[None], grad_down[None]


def solution(mesh):
    fine = Mesh(mesh.devices.reshape(2, YLO, Z, X, CORES), AXES)
    wide, narrow = WIDE_AXES, ("x", "core")
    return jax.shard_map(
        body,
        mesh=fine,
        in_specs=(
            P("section", None, narrow),
            P(wide, narrow),
            P("section", narrow, wide),
            P("section", wide, narrow),
        ),
        out_specs=(
            P("section", wide, narrow),
            P("section", narrow, wide),
            P("section", wide, narrow),
        ),
        check_vma=False,
    )
```

```python
import jax
import jax.numpy as jnp
from jax import lax
from jax.sharding import Mesh, PartitionSpec as P

gelu_scale = 0.7978845608028654
cubic_term = 0.044715

X, CORES, YLO, Z = 4, 2, 2, 8
WIDE = YLO * Z
AXES = ("section", "ylo", "z", "x", "core")
WIDE_AXES = ("ylo", "z")
CROSS_AXES = ("section", "ylo")


def gelu_parts(pre_act):
    inner = jnp.tanh(gelu_scale * (pre_act + cubic_term * pre_act * pre_act * pre_act))
    act_value = 0.5 * pre_act * (1.0 + inner)
    slopes = 0.5 * (1.0 + inner) + 0.5 * pre_act * (1.0 - inner * inner) * gelu_scale * (
        1.0 + 3.0 * cubic_term * pre_act * pre_act
    )
    return (act_value, slopes)


def contract(first_op, second_op, first_dim, second_dim):
    return lax.dot_general(
        first_op,
        second_op,
        (((first_dim,), (second_dim,)), ((), ())),
        preferred_element_type=jnp.float32,
    )


def together(*values):
    return lax.optimization_barrier(values)


def other_core(block):
    return lax.ppermute(block, "core", [(0, 1), (1, 0)])


def to_upper(block):
    return lax.ppermute(block, CROSS_AXES, [(0, 3), (1, 2)])


def to_lower(block):
    return lax.ppermute(block, CROSS_AXES, [(3, 0), (2, 1)])


def halves(weight, dim):
    size = weight.shape[dim] // CORES
    core = lax.axis_index("core")
    return (
        lax.dynamic_slice_in_dim(weight, core * size, size, dim),
        lax.dynamic_slice_in_dim(weight, (1 - core) * size, size, dim),
    )


def in_order(mine, theirs):
    first = lax.axis_index("core") == 0
    return jnp.concatenate(
        [jnp.where(first, mine, theirs), jnp.where(first, theirs, mine)], axis=1
    )


def pair_sum(mine, theirs):
    return mine + other_core(theirs.astype(jnp.bfloat16)).astype(jnp.float32)


def step_x(block, distance):
    return lax.ppermute(block, "x", [(i, (i + distance) % X) for i in range(X)])


def narrow_terms(pair):
    sent = pair.astype(jnp.bfloat16)
    return [pair] + [step_x(sent, distance) for distance in (1, 3, 2)]


def spread_x(partial):
    rows, cols = partial.shape
    x = lax.axis_index("x")
    blocks = partial.reshape(X, rows // X, cols)
    total = lax.dynamic_index_in_dim(blocks, x, 0, keepdims=False)
    sent = blocks.astype(jnp.bfloat16)
    for distance in (1, 3, 2):
        block = lax.dynamic_index_in_dim(sent, lax.rem(x + distance, X), 0, keepdims=False)
        total = total + step_x(block, distance).astype(jnp.float32)
    return total


def send_x(block):
    return [block] + [step_x(block, distance) for distance in (1, 2, 3)]


def place_x(found):
    rows, cols = found[0].shape
    source = lax.broadcasted_iota(jnp.int32, (X, 1, 1), 0)
    passed = lax.rem(lax.axis_index("x") - source + X, X)
    placed = found[0][None]
    for distance in (1, 2, 3):
        placed = jnp.where(passed == distance, found[distance][None], placed)
    return placed.reshape(X * rows, cols)


def add_terms(terms):
    return sum(term.astype(jnp.float32) for term in terms)


def spread_wide(partial):
    rows, cols = partial.shape
    return lax.all_to_all(
        partial.reshape(WIDE, rows // WIDE, cols), WIDE_AXES, 0, 0, tiled=True
    )


def add_blocks(blocks):
    return jnp.sum(blocks.astype(jnp.float32), axis=0)


def gather_wide(block):
    rows, cols = block.shape
    return lax.all_to_all(
        jnp.broadcast_to(block[None], (WIDE, rows, cols)), WIDE_AXES, 0, 0, tiled=True
    ).reshape(WIDE * rows, cols)


def back_total(whole, down_halves):
    theirs = contract(whole, down_halves[1], 1, 1)
    mine = contract(whole, down_halves[0], 1, 1)
    return add_terms(narrow_terms(pair_sum(mine, theirs)))


def slope_of(total, slopes):
    mine = (total * slopes).astype(jnp.bfloat16)
    return mine, other_core(mine)


def back_through_up(slope, up_halves):
    return (contract(slope[0], up_halves[0], 1, 1) + contract(slope[1], up_halves[1], 1, 1)).astype(
        jnp.bfloat16
    )


def body(saved_inputs, upstream, up_weight, down_weight):
    is_upper = lax.axis_index("section") == 1

    def pick(upper, lower):
        return jnp.where(is_upper, upper, lower)

    def by_part(block):
        rows, cols = block.shape
        split = block.reshape(WIDE, 2, rows // (2 * WIDE), cols)
        return [split[:, c].reshape(rows // 2, cols) for c in range(2)]

    w_up, w_down = up_weight[0], down_weight[0]
    up_halves, down_halves = halves(w_up, 1), halves(w_down, 0)
    saved = by_part(saved_inputs[0])
    first, last = slice(0, saved[0].shape[0]), slice(saved[0].shape[0], None)

    sent_down = to_upper(w_down)

    theirs = jnp.concatenate([contract(rows, up_halves[1], 1, 0) for rows in saved], axis=0)
    mine = jnp.concatenate([contract(rows, up_halves[0], 1, 0) for rows in saved], axis=0)
    act, slopes = gelu_parts(spread_x(pair_sum(mine, theirs)))
    act = act.astype(jnp.bfloat16)
    slopes = place_x(send_x(slopes.astype(jnp.bfloat16)))
    gathered, act = together(gather_wide(upstream), act)

    top = by_part(gathered)
    theirs = contract(top[0], down_halves[1], 1, 1)
    mine = contract(top[0], down_halves[0], 1, 1)
    mine, slopes = together(mine, slopes)
    top_slope = slope_of(add_terms(narrow_terms(pair_sum(mine, theirs))), slopes[first])
    moved = to_lower(back_through_up(top_slope, up_halves))
    late_slopes, _ = together(slopes[last], top_slope[0])
    top_slope_rest = slope_of(back_total(top[1], down_halves), late_slopes)
    partial = pick(back_through_up(top_slope_rest, up_halves), moved)
    half = w_up.shape[0] // 2
    sent_up = [to_upper(together(w_up[:half], sent_down)[0])]
    sent_up.append(to_upper(together(w_up[half:], sent_up[0])[0]))
    partial, act = together(partial, act)
    own = in_order(act, other_core(act))
    blocks, lower_slopes, _ = together(spread_wide(partial), to_upper(slopes[last]), own)
    low_down = pick(sent_down, w_down)
    part = upstream.shape[0] // 2
    middle = (
        pick(upstream[part:], upstream[:part]).astype(jnp.float32) + add_blocks(blocks)
    ).astype(jnp.bfloat16)

    hidden = send_x(own)
    low = gather_wide(middle)
    lower_slopes = pick(lower_slopes, slopes[first])
    low_rest = to_lower(low)
    low_halves = halves(low_down, 0)
    theirs = contract(low, low_halves[1], 1, 1)
    mine = contract(low, low_halves[0], 1, 1)
    hidden[0], theirs = together(hidden[0], theirs)
    pair, hidden = together(pair_sum(mine, theirs), place_x(hidden))
    low_total = add_terms(narrow_terms(pair))
    incoming = jnp.concatenate([pick(top[0], low), pick(top[1], low_rest)], axis=0)
    grad_down = contract(hidden, incoming, 0, 0).astype(jnp.bfloat16)
    low_up = [pick(sent_up[0], w_up[:half])]
    low_total, grad_down, sent_up[1], low_up[0] = together(
        low_total, grad_down, sent_up[1], low_up[0]
    )
    low_up.append(pick(sent_up[1], w_up[half:]))
    low_slope = slope_of(low_total, lower_slopes)
    low_slope_rest = to_lower(low_slope[0])
    low_blocks = spread_wide(
        jnp.concatenate([back_through_up(low_slope, halves(piece, 1)) for piece in low_up], axis=1)
    )
    slope_grad = jnp.concatenate(
        [
            in_order(*[pick(u, l) for u, l in zip(top_slope, low_slope)]),
            in_order(
                pick(top_slope_rest[0], low_slope_rest),
                pick(top_slope_rest[1], other_core(low_slope_rest)),
            ),
        ],
        axis=0,
    )
    grad_up = contract(jnp.concatenate(saved, axis=0), slope_grad, 0, 0).astype(jnp.bfloat16)
    low_blocks, grad_up = together(low_blocks, grad_up)
    bottom = (middle.astype(jnp.float32) + add_blocks(low_blocks)).astype(jnp.bfloat16)

    swap = [(0, 1), (1, 0)]
    upper_first = lax.ppermute(middle, "section", swap)
    lower_last = lax.ppermute(bottom, "section", swap)
    grad_in = jnp.concatenate([pick(upper_first, bottom), pick(middle, lower_last)], axis=0)
    return grad_in[None], grad_up[None], grad_down[None]


def solution(mesh):
    fine = Mesh(mesh.devices.reshape(2, YLO, Z, X, CORES), AXES)
    wide, narrow = WIDE_AXES, ("x", "core")
    return jax.shard_map(
        body,
        mesh=fine,
        in_specs=(
            P("section", None, narrow),
            P(wide, narrow),
            P("section", narrow, wide),
            P("section", wide, narrow),
        ),
        out_specs=(
            P("section", wide, narrow),
            P("section", narrow, wide),
            P("section", wide, narrow),
        ),
        check_vma=False,
    )
```
